32 devices in a mesh: gx: 8 (over y, x, core), gy: 4 (over z).
Axes of the slice: x: 2, y: 2, z: 4, core: 2. Of those that a mesh axis runs over, the one named last changes fastest.
Arguments:
- velocity: float32 [3, 512, 64, 512], P(None, 'gx', None, 'gy'), may hold values from -6 to 6
- cotangent: float32 [3, 512, 64, 512], P(None, 'gx', None, 'gy'), may hold values from -6 to 6
- coefficient: float32 [512, 64, 512], P('gx', None, 'gy'), may hold values from 0.5 to 1.5
- level_profile: float32 [64], replicated, may hold values from 0.1 to 1
- vert_deriv: float32 [64, 64], replicated, may hold values from -0.75 to 0.75
- eigen_vectors: float32 [64, 64], replicated, may hold values from -0.75 to 0.75
- eigen_inverse: float32 [64, 64], replicated, may hold values from -0.75 to 0.75
- eigen_rates: float32 [64], replicated, may hold values from 0.25 to 4
Outputs:
- new_velocity: float32 [3, 512, 64, 512], P(None, 'gx', None, 'gy')
- adjoint_velocity: float32 [3, 512, 64, 512], P(None, 'gx', None, 'gy')
- viscosity_gradient: float32 [512, 64, 512], P('gx', None, 'gy')
The draws below stay inside these ranges and needn't reach their ends.
All inputs are finite; a program needn't handle non-finite values.
Results may differ from the reference program's by a relative error of at most 0.00005.
Values sent between devices are 32-bit elements; how exact they have to be, the bound alone decides.
No kernel may reach another device: no remote copies, remote signals or barrier semaphores. Data moves between devices by JAX's collectives and lax.ppermute only.
A program may use at most 256 MiB of HBM per device.

```python
import math
import jax
import jax.numpy as jnp
from jax import lax

NX = 512
NY = 512
NZ = 64


def level_of(stream_key, dims, pieces, smallest, largest):
    def one(position, blocks):
        heights = jax.random.uniform(jax.random.fold_in(jax.random.fold_in(stream_key, 6), position), (blocks,), jnp.float32, smallest / len(pieces), largest / len(pieces))
        return jnp.repeat(jnp.exp(heights), dims[position] // blocks).reshape((-1,) + (1,) * (len(dims) - position - 1))

    loudness = one(*pieces[0])
    for cut in pieces[1:]:
        loudness = loudness * one(*cut)
    return loudness


def gaussian(rng, dims, deviation, limit, split=(), kind=jnp.bfloat16):
    array = deviation * jax.random.normal(rng, dims, jnp.float32)
    if split:
        array = array * level_of(rng, dims, split, -0.22, 0.18)
    return jnp.clip(array, -limit, limit).astype(kind)


def setup_inputs(seed: int = 0) -> dict:
    arg_keys = jax.random.split(jax.random.key(seed), 9)
    velocity = gaussian(arg_keys[0], (3, NX, NZ, NY), 1.0, 6.0, ((1, 8), (3, 4)), jnp.float32)
    cotangent = gaussian(arg_keys[1], (3, NX, NZ, NY), 1.0, 6.0, ((1, 8), (3, 4)), jnp.float32)
    coefficient = jnp.clip(0.5 + 1.0 * jax.random.uniform(arg_keys[2], (NX, NZ, NY), jnp.float32) ** level_of(arg_keys[2], (NX, NZ, NY), ((0, 8), (2, 4)), -0.2, 0.2), 0.5, 1.5)
    level_profile = jnp.clip(jnp.exp(jax.random.uniform(arg_keys[3], (NZ,), jnp.float32, math.log(0.1), math.log(1.0))), 0.1, 1.0)
    vert_deriv = gaussian(arg_keys[4], (NZ, NZ), NZ ** -0.5, 0.75, (), jnp.float32)
    eigen_vectors = gaussian(arg_keys[5], (NZ, NZ), NZ ** -0.5, 0.75, (), jnp.float32)
    eigen_inverse = gaussian(arg_keys[6], (NZ, NZ), NZ ** -0.5, 0.75, (), jnp.float32)
    eigen_rates = jnp.clip(jnp.exp(jax.random.uniform(arg_keys[7], (NZ,), jnp.float32, math.log(0.25), math.log(4.0))), 0.25, 4.0)
    return dict(velocity=velocity, cotangent=cotangent, coefficient=coefficient, level_profile=level_profile, vert_deriv=vert_deriv, eigen_vectors=eigen_vectors, eigen_inverse=eigen_inverse, eigen_rates=eigen_rates)


step_weight = 0.3 * 8.0 / 15.0
precise = lax.Precision.HIGHEST


def levels(matrix, field):
    return jnp.einsum('mz,xzy->xmy', matrix, field, precision=precise)


def wavenumbers(count):
    modes = jnp.arange(count, dtype=jnp.int32)
    signed = jnp.where(modes < count // 2, modes, modes - count)
    signed = jnp.where(modes == count // 2, jnp.zeros_like(signed), signed)
    return signed.astype(jnp.float32) * (2.0 * math.pi / count)


def spectral(fields, eigen_rates):
    spectra = jnp.fft.fft2(fields, axes=(1, 3))
    wave_x = wavenumbers(NX)[:, None, None]
    wave_y = wavenumbers(NY)[None, None, :]
    diverg = 1j * wave_x * spectra[0] + 1j * wave_y * spectra[1] + spectra[2]
    factor = -1.0 / (eigen_rates[None, :, None] + wave_x * wave_x + wave_y * wave_y)
    solved = factor * diverg
    terms = jnp.stack([1j * wave_x * solved, 1j * wave_y * solved, solved])
    inverse = jnp.fft.ifft2(terms, axes=(1, 3))
    return jnp.real(inverse).astype(fields.dtype)


def reference(velocity, cotangent, coefficient, level_profile, vert_deriv, eigen_vectors, eigen_inverse, eigen_rates):
    east = jnp.roll(velocity, -1, axis=1)
    west = jnp.roll(velocity, 1, axis=1)
    north = jnp.roll(velocity, -1, axis=3)
    south = jnp.roll(velocity, 1, axis=3)
    slope_x = 0.5 * (east - west)
    slope_y = 0.5 * (north - south)
    laplace = east + west + north + south - 4.0 * velocity
    slope_z = jnp.einsum('mz,cxzy->cxmy', vert_deriv, velocity, precision=precise)
    advect = -(velocity[0] * slope_x + velocity[1] * slope_y + velocity[2] * slope_z)
    viscosity = coefficient * level_profile[None, :, None]
    section = velocity + step_weight * (advect + viscosity * laplace)
    forward_in = jnp.stack([levels(eigen_inverse, section[0]), levels(eigen_inverse, section[1]),
                            levels(eigen_inverse, levels(vert_deriv, section[2]))])
    forward_out = spectral(forward_in, eigen_rates)
    pressure = jnp.stack([levels(eigen_vectors, forward_out[0]), levels(eigen_vectors, forward_out[1]),
                          levels(vert_deriv, levels(eigen_vectors, forward_out[2]))])
    new_velocity = section - pressure
    vectors_t = eigen_vectors.T
    inverse_t = eigen_inverse.T
    deriv_t = vert_deriv.T
    adjoint_in = jnp.stack([-levels(vectors_t, cotangent[0]), -levels(vectors_t, cotangent[1]),
                            levels(vectors_t, levels(deriv_t, cotangent[2]))])
    adjoint_out = spectral(adjoint_in, eigen_rates)
    adjoint_velocity = cotangent + jnp.stack([levels(inverse_t, adjoint_out[0]), levels(inverse_t, adjoint_out[1]),
                                              -levels(deriv_t, levels(inverse_t, adjoint_out[2]))])
    gradient = step_weight * level_profile[None, :, None] * jnp.sum(adjoint_velocity * laplace, axis=0)
    return new_velocity, adjoint_velocity, gradient
```

```python
import functools
import math

import jax
import jax.numpy as jnp
import numpy as np
from jax import lax
from jax.experimental import pallas as pl
from jax.experimental.pallas import tpu as pltpu
from jax.sharding import PartitionSpec as P

step_weight = 0.3 * 8.0 / 15.0
precise = lax.Precision.HIGHEST
half = jnp.bfloat16
vmem_bytes = 60 * 1024 * 1024


def line_transform(count):
    modes = count // 2
    points = np.arange(count)
    angle = (np.arange(modes)[:, None] * points[None, :] % count) * (2.0 * np.pi / count)
    real = np.cos(angle)
    imag = -np.sin(angle)
    imag[0] = np.where(points % 2 == 0, 1.0, -1.0)
    scale = np.full((modes, 1), 2.0 / count)
    scale[0] = 1.0 / count
    wave = (np.arange(modes) * (2.0 * np.pi / count))[:, None]
    forward = np.stack([real, imag])
    forward_slope = np.stack([-wave * imag, wave * real])
    inverse = np.stack([scale * real, scale * imag])
    inverse_slope = np.stack([scale * wave * imag, -scale * wave * real])
    return forward, forward_slope, inverse, inverse_slope


def grouped(table, groups):
    parts, modes, points = table.shape
    split = table.reshape(parts, groups, modes // groups, points)
    return np.swapaxes(split, 0, 1).reshape(groups, parts * modes // groups, points)


def halves(table):
    table = table.astype(np.float32)
    high = table.astype(half)
    low = (table - high.astype(np.float32)).astype(half)
    return np.stack([high, low])


def split(values):
    high = values.astype(half)
    low = (values - high.astype(jnp.float32)).astype(half)
    return high, low


def product(left, right):
    def dot(a, b):
        return jnp.dot(a, b, preferred_element_type=jnp.float32)

    return dot(left[0], right[0]) + (dot(left[0], right[1]) + dot(left[1], right[0]))


def parameters(flops, read, written):
    return dict(
        compiler_params=pltpu.CompilerParams(vmem_limit_bytes=vmem_bytes),
        cost_estimate=pl.CostEstimate(
            flops=100 * flops, bytes_accessed=400 * (read + written), transcendentals=0
        ),
    )


def block_x(part_x):
    return 16 if part_x % 16 == 0 else 8


def wide(matrix):
    high = lax.reduce_precision(matrix, exponent_bits=8, mantissa_bits=7)
    low = (matrix - high).astype(half)
    high = high.astype(half)
    return jnp.concatenate([high, high, low], axis=-1)


def narrow_product(matrix, field):
    high, low = split(field)
    return jnp.dot(
        matrix, jnp.concatenate([high, low, high], axis=0), preferred_element_type=jnp.float32
    )


anywhere = pl.BlockSpec(memory_space=pl.ANY)
scalars = pl.BlockSpec(memory_space=pltpu.SMEM)


def into_kernel(field_ref, matrix_ref, *refs):
    out_ref, rows_ref = refs[-2:]
    sublanes, levels, part_y = field_ref.shape[1:]
    for pair in range(0, sublanes, 2):
        fields = jnp.concatenate([field_ref[0, pair], field_ref[0, pair + 1]], axis=1)
        turned = narrow_product(matrix_ref[0], fields)
        for x in (pair, pair + 1):
            rows_ref[pl.ds(x, levels, stride=sublanes), :] = turned[
                :, (x - pair) * part_y : (x - pair + 1) * part_y
            ]
    out_ref[...] = rows_ref[...].reshape(out_ref.shape)


def into_levels(fields, matrices, components, groups, *follow):
    _, part_x, levels, part_y = fields.shape
    sublanes = block_x(part_x)
    count = len(components)
    per = levels // groups
    first, step = components[0], (components[1] - components[0] if count > 1 else 1)
    size = count * part_x * levels * part_y
    return pl.pallas_call(
        into_kernel,
        grid=(count, part_x // sublanes),
        in_specs=[
            pl.BlockSpec(
                (1, sublanes, levels, part_y), lambda f, i: (first + f * step, i, 0, 0)
            ),
            pl.BlockSpec((1, levels, 3 * levels), lambda f, i: (f, 0, 0)),
        ]
        + [anywhere] * len(follow),
        out_specs=pl.BlockSpec((groups, 1, per, sublanes, part_y), lambda f, i: (0, f, 0, i, 0)),
        out_shape=jax.ShapeDtypeStruct((groups, count, per, part_x, part_y), jnp.float32),
        scratch_shapes=[pltpu.VMEM((levels * sublanes, part_y), jnp.float32)],
        name="into_levels",
        **parameters(6 * size * levels, size, size),
    )(fields, wide(matrices), *follow)


def edges_kernel(field_ref, _, low_ref, high_ref, first_ref, last_ref):
    sublanes, levels, part_y = field_ref.shape[1:]
    step = pl.program_id(0)
    lane = lax.broadcasted_iota(jnp.int32, (levels, low_ref.shape[2]), 1)
    for c in range(3):
        low = low_ref[c]
        high = high_ref[c]
        for x in range(sublanes):
            here = lane == step * sublanes + x
            low = jnp.where(here, field_ref[c, x, :, 0:1], low)
            high = jnp.where(here, field_ref[c, x, :, part_y - 1 : part_y], high)
        low_ref[c] = low
        high_ref[c] = high

    @pl.when(step == 0)
    def _():
        first_ref[...] = field_ref[:, 0:1]

    @pl.when(step == pl.num_programs(0) - 1)
    def _():
        last_ref[...] = field_ref[:, sublanes - 1 :]


def edges_of(field, follow):
    _, part_x, levels, part_y = field.shape
    sublanes = block_x(part_x)
    size = part_x * levels * part_y
    shapes = [(3, levels, part_x)] * 2 + [(3, 1, levels, part_y)] * 2
    return pl.pallas_call(
        edges_kernel,
        grid=(part_x // sublanes,),
        in_specs=[
            pl.BlockSpec((3, sublanes, levels, part_y), lambda i: (0, i, 0, 0)),
            anywhere,
        ],
        out_specs=[pl.BlockSpec(shapes[0], lambda i: (0, 0, 0))] * 2
        + [pl.BlockSpec(shapes[2], lambda i: (0, 0, 0, 0))] * 2,
        out_shape=[jax.ShapeDtypeStruct(shape, jnp.float32) for shape in shapes],
        name="edges_of",
        **parameters(0, 3 * size, 0),
    )(field, follow)


def section_kernel(*refs):
    field_ref, own_ref, before_ref, after_ref, west_ref, east_ref, south_ref, north_ref = refs[:8]
    coefficient_ref, profile_ref, deriv_ref, matrix_ref = refs[8:12]
    section_ref, laplace_ref, out_ref, rows_ref = refs[-4:]
    sublanes, levels, part_y = field_ref.shape[1:]
    edges = south_ref.shape[2]
    step = pl.program_id(1)
    last = pl.num_programs(1) - 1
    lane = lax.broadcasted_iota(jnp.int32, (levels, part_y), 1)
    profile = step_weight * profile_ref[...]
    for pair in range(0, sublanes, 2):
        own = jnp.concatenate([own_ref[0, pair], own_ref[0, pair + 1]], axis=1)
        slopes = narrow_product(deriv_ref[...], own)
        sections = []
        for x in (pair, pair + 1):
            place = step * sublanes + x
            field = own_ref[0, x]
            if x == 0:
                west = jnp.where(step == 0, west_ref[0, 0], before_ref[0, 0])
            else:
                west = own_ref[0, x - 1]
            if x == sublanes - 1:
                east = jnp.where(step == last, east_ref[0, 0], after_ref[0, 0])
            else:
                east = own_ref[0, x + 1]
            low = pltpu.roll(south_ref[0], lax.rem(edges - place, edges), 1)[:, :part_y]
            high = pltpu.roll(north_ref[0], lax.rem(edges + part_y - 1 - place, edges), 1)
            south = jnp.where(lane == 0, low, pltpu.roll(field, 1, 1))
            north = jnp.where(
                lane == part_y - 1, high[:, :part_y], pltpu.roll(field, part_y - 1, 1)
            )
            laplace = east + west + north + south - 4.0 * field
            slope_z = slopes[:, (x - pair) * part_y : (x - pair + 1) * part_y]
            advect = (0.5 * field_ref[0, x]) * (east - west)
            advect = advect + (0.5 * field_ref[1, x]) * (north - south)
            advect = advect + field_ref[2, x] * slope_z
            viscosity = profile * coefficient_ref[x]
            section = field + (viscosity * laplace - step_weight * advect)
            laplace_ref[0, x] = laplace
            section_ref[0, x] = section
            sections.append(section)
        turned = narrow_product(matrix_ref[0], jnp.concatenate(sections, axis=1))
        for x in (pair, pair + 1):
            rows_ref[pl.ds(x, levels, stride=sublanes), :] = turned[
                :, (x - pair) * part_y : (x - pair + 1) * part_y
            ]
    out_ref[...] = rows_ref[...].reshape(out_ref.shape)


def make_section(
    field, sides, edges, coefficient, profile, deriv, matrices, groups, components, done, follow
):
    _, part_x, levels, part_y = field.shape
    sublanes = block_x(part_x)
    per = levels // groups
    count = len(components)
    first, step = components[0], (components[1] - components[0] if count > 1 else 1)
    size = count * part_x * levels * part_y
    whole = pl.BlockSpec((3, sublanes, levels, part_y), lambda f, i: (0, i, 0, 0))
    own = pl.BlockSpec((1, sublanes, levels, part_y), lambda f, i: (first + f * step, i, 0, 0))
    plane = (1, 1, levels, part_y)
    fixed = pl.BlockSpec(plane, lambda f, i: (first + f * step, 0, 0, 0))
    edge = pl.BlockSpec((1, *edges[0].shape[1:]), lambda f, i: (first + f * step, 0, 0))
    full = jax.ShapeDtypeStruct(field.shape, jnp.float32)
    return pl.pallas_call(
        section_kernel,
        grid=(count, part_x // sublanes),
        in_specs=[
            whole,
            own,
            pl.BlockSpec(
                plane, lambda f, i: (first + f * step, jnp.maximum(i * sublanes - 1, 0), 0, 0)
            ),
            pl.BlockSpec(
                plane,
                lambda f, i: (
                    first + f * step,
                    jnp.minimum((i + 1) * sublanes, part_x - 1),
                    0,
                    0,
                ),
            ),
            fixed,
            fixed,
            edge,
            edge,
            pl.BlockSpec((sublanes, levels, part_y), lambda f, i: (i, 0, 0)),
            pl.BlockSpec((levels, part_y), lambda f, i: (0, 0)),
            pl.BlockSpec((levels, 3 * levels), lambda f, i: (0, 0)),
            pl.BlockSpec((1, levels, 3 * levels), lambda f, i: (f, 0, 0)),
        ]
        + [anywhere] * (len(done) + len(follow)),
        out_specs=[
            own,
            own,
            pl.BlockSpec((groups, 1, per, sublanes, part_y), lambda f, i: (0, f, 0, i, 0)),
        ],
        out_shape=[
            full,
            full,
            jax.ShapeDtypeStruct((groups, count, per, part_x, part_y), jnp.float32),
        ],
        input_output_aliases={12 + i: i for i in range(len(done))},
        scratch_shapes=[pltpu.VMEM((levels * sublanes, part_y), jnp.float32)],
        name="make_section",
        **parameters(12 * size * levels, 6 * size, 3 * size),
    )(
        field,
        field,
        field,
        field,
        *sides,
        *edges,
        coefficient,
        profile,
        wide(deriv),
        wide(matrices),
        *done,
        *follow,
    )


def x_kernel(me_ref, rows_ref, table_ref, *refs):
    targets = table_ref.shape[1]
    out_refs = refs[-targets:]
    groups, count, block, part_x, part_y = rows_ref.shape
    columns = []
    for m in range(block):
        lines = [rows_ref[:, f, m].reshape(groups * part_x, part_y) for f in range(count)]
        columns.append(jnp.concatenate(lines, axis=0))
    data = split(jnp.concatenate(columns, axis=1))
    for s, out_ref in enumerate(out_refs):
        target = lax.rem(me_ref[0] + s, targets)
        spectrum = product((table_ref[0, target], table_ref[1, target]), data)
        for m in range(block):
            out_ref[m] = spectrum[:, m * part_y : (m + 1) * part_y]


def block_of(levels):
    return 2 if levels % 2 == 0 else 1


def x_forward(me, rows, table, *follow):
    groups, count, levels, part_x, part_y = rows.shape
    targets, lines, depth = table.shape[1:]
    block = block_of(levels)
    size = groups * count * levels * part_x * part_y
    return pl.pallas_call(
        x_kernel,
        grid=(levels // block,),
        in_specs=[
            scalars,
            pl.BlockSpec((groups, count, block, part_x, part_y), lambda i: (0, 0, i, 0, 0)),
            pl.BlockSpec(table.shape, lambda i: (0, 0, 0, 0)),
        ]
        + [anywhere] * len(follow),
        out_specs=[pl.BlockSpec((block, lines, part_y), lambda i: (i, 0, 0))] * targets,
        out_shape=[jax.ShapeDtypeStruct((levels, lines, part_y), jnp.float32)] * targets,
        name="x_forward",
        **parameters(6 * size * targets * lines, size + table.size // 2, size // count),
    )(me, rows, table, *follow)


def solve_kernel(sources, full, group_ref, rates_ref, _, *refs):
    full_x, full_y = full
    in_refs = refs[: 2 * sources]
    forward_ref, inverse_ref = refs[2 * sources : 2 * sources + 2]
    out_refs = refs[2 * sources + 2 :]
    block, lines, part_y = in_refs[0].shape
    me = group_ref[0]
    data = split(
        jnp.concatenate([ref[...].reshape(block * lines, part_y) for ref in in_refs], axis=1)
    )
    origins = [lax.rem(me + sources - s, sources) for s in range(sources)]
    diverg = product(
        data,
        [
            jnp.concatenate([forward_ref[h, p, o] for p in range(2) for o in origins], axis=0)
            for h in range(2)
        ],
    )
    shape = (lines, full_y)
    pairs = lines // 2
    mode_x = me * pairs + lax.broadcasted_iota(jnp.int32, shape, 0) % pairs
    mode_y = lax.broadcasted_iota(jnp.int32, shape, 1) % (full_y // 2)
    wave_x = mode_x.astype(jnp.float32) * (2.0 * math.pi / full_x)
    wave_y = mode_y.astype(jnp.float32) * (2.0 * math.pi / full_y)
    squares = wave_x * wave_x + wave_y * wave_y
    solved = []
    for m in range(block):
        rate = rates_ref[pl.program_id(0) * block + m]
        solved.append(-diverg[m * lines : (m + 1) * lines] / (rate + squares))
    solved = split(jnp.concatenate(solved, axis=0))
    for s, out_ref in enumerate(out_refs):
        place = (s // sources, lax.rem(me + s, sources))
        result = product(solved, (inverse_ref[(0, *place)], inverse_ref[(1, *place)]))
        out_ref[...] = result.reshape(block, lines, part_y)


def y_solve(plain, sloped, rates, group, forward, inverse, full, follow):
    levels, lines, part_y = plain[0].shape
    sources = len(plain)
    block = block_of(levels)
    size = levels * lines * part_y * sources
    targets = 2 * sources
    spec = pl.BlockSpec((block, lines, part_y), lambda i: (i, 0, 0))
    fixed = pl.BlockSpec(forward.shape, lambda i: (0, 0, 0, 0, 0))
    outs = pl.pallas_call(
        functools.partial(solve_kernel, sources, full),
        grid=(levels // block,),
        in_specs=[scalars, scalars, anywhere]
        + [spec] * (2 * sources)
        + [fixed, pl.BlockSpec(inverse.shape, lambda i: (0, 0, 0, 0, 0))],
        out_specs=[spec] * targets,
        out_shape=[jax.ShapeDtypeStruct((levels, lines, part_y), jnp.float32)] * targets,
        name="y_solve",
        **parameters(
            24 * size * full[1], 2 * size + forward.size // 2 + inverse.size // 2, 2 * size
        ),
    )(group, rates, follow, *plain, *sloped, forward, inverse)
    return outs[:sources], outs[sources:]


def x_inverse_kernel(sources, me_ref, _, *refs):
    in_refs = refs[:sources]
    table_ref, out_ref, high_ref, low_ref, rows_ref = refs[sources:]
    _, _, part_x, levels, part_y = out_ref.shape

    @pl.when((pl.program_id(0) == 0) & (pl.program_id(1) == 0))
    def _():
        for m in range(levels):
            high, low = split(jnp.concatenate([ref[m] for ref in in_refs], axis=0))
            high_ref[:, m * part_y : (m + 1) * part_y] = high
            low_ref[:, m * part_y : (m + 1) * part_y] = low

    origins = [lax.rem(me_ref[0] + sources - s, sources) for s in range(sources)]
    table = [
        jnp.concatenate([table_ref[h, 0, o] for o in origins], axis=1) for h in range(2)
    ]
    lines = table[0].shape[0]
    for m in range(levels):
        cut = slice(m * part_y, (m + 1) * part_y)
        rows_ref[pl.ds(m, lines, stride=levels), :] = product(
            table, (high_ref[:, cut], low_ref[:, cut])
        )
    out_ref[...] = rows_ref[...].reshape(out_ref.shape)


def x_inverse(me, pieces, table, groups, follow):
    sources = len(pieces)
    levels, lines, part_y = pieces[0].shape
    count, full_x = table.shape[1], table.shape[3]
    part_x = full_x // groups
    steps = 2 if groups % 2 == 0 else 1
    rows = full_x // steps
    size = levels * full_x * part_y
    return pl.pallas_call(
        functools.partial(x_inverse_kernel, sources),
        grid=(count, steps),
        in_specs=[scalars, anywhere]
        + [pl.BlockSpec((levels, lines, part_y), lambda f, i: (0, 0, 0))] * sources
        + [pl.BlockSpec((2, 1, sources, rows, lines), lambda f, i: (0, f, 0, i, 0))],
        out_specs=pl.BlockSpec(
            (groups // steps, 1, part_x, levels, part_y), lambda f, i: (i, f, 0, 0, 0)
        ),
        out_shape=jax.ShapeDtypeStruct((groups, count, part_x, levels, part_y), jnp.float32),
        scratch_shapes=[pltpu.VMEM((full_x, levels * part_y), half)] * 2
        + [pltpu.VMEM((rows * levels, part_y), jnp.float32)],
        name="x_inverse",
        **parameters(6 * size * full_x * count, size + table.size // 2, size * count),
    )(me, follow, *pieces, table)


def column(rows_ref, component, x):
    groups = rows_ref.shape[0]
    return jnp.concatenate([rows_ref[g, component, x] for g in range(groups)], axis=0)


def from_kernel(rows_ref, matrix_ref, base_ref, out_ref):
    part_y = base_ref.shape[3]
    for pair in range(0, base_ref.shape[1], 2):
        fields = [column(rows_ref, 0, x) for x in (pair, pair + 1)]
        turned = narrow_product(matrix_ref[0], jnp.concatenate(fields, axis=1))
        out_ref[0, pair] = base_ref[0, pair] + turned[:, :part_y]
        out_ref[0, pair + 1] = base_ref[0, pair + 1] + turned[:, part_y:]


def from_levels(rows, matrices, base, components, in_place):
    groups, count, part_x, per, part_y = rows.shape
    levels = groups * per
    sublanes = block_x(part_x)
    first, step = components[0], (components[1] - components[0] if count > 1 else 1)
    size = count * part_x * levels * part_y
    spec = pl.BlockSpec((1, sublanes, levels, part_y), lambda f, i: (first + f * step, i, 0, 0))
    return pl.pallas_call(
        from_kernel,
        grid=(count, part_x // sublanes),
        in_specs=[
            pl.BlockSpec((groups, 1, sublanes, per, part_y), lambda f, i: (0, f, i, 0, 0)),
            pl.BlockSpec((1, levels, 3 * levels), lambda f, i: (f, 0, 0)),
            spec,
        ],
        out_specs=spec,
        out_shape=jax.ShapeDtypeStruct(base.shape, jnp.float32),
        input_output_aliases={2: 0} if in_place else {},
        name="from_levels",
        **parameters(6 * size * levels, 2 * size, size),
    )(rows, wide(matrices), base)


def gradient_kernel(
    rows_ref, matrix_ref, base_ref, done_ref, laplace_ref, profile_ref, _, out_ref, gradient_ref
):
    profile = step_weight * profile_ref[...]
    part_y = base_ref.shape[3]
    for pair in range(0, base_ref.shape[1], 2):
        fields = [column(rows_ref, 0, x) for x in (pair, pair + 1)]
        turned = narrow_product(matrix_ref[0], jnp.concatenate(fields, axis=1))
        for x in (pair, pair + 1):
            value = base_ref[0, x] + turned[:, (x - pair) * part_y : (x - pair + 1) * part_y]
            first, last = done_ref[0, x], done_ref[2, x]
            out_ref[0, x], out_ref[1, x], out_ref[2, x] = first, value, last
            total = first * laplace_ref[0, x] + value * laplace_ref[1, x]
            gradient_ref[x] = profile * (total + last * laplace_ref[2, x])


def gradient_of(rows, matrix, base, done, laplace, profile, follow):
    groups, _, part_x, per, part_y = rows.shape
    levels = groups * per
    sublanes = block_x(part_x)
    size = part_x * levels * part_y

    whole = pl.BlockSpec((3, sublanes, levels, part_y), lambda i: (0, i, 0, 0))
    return pl.pallas_call(
        gradient_kernel,
        grid=(part_x // sublanes,),
        in_specs=[
            pl.BlockSpec((groups, 1, sublanes, per, part_y), lambda i: (0, 0, i, 0, 0)),
            pl.BlockSpec((1, levels, 3 * levels), lambda i: (0, 0, 0)),
            pl.BlockSpec((1, sublanes, levels, part_y), lambda i: (1, i, 0, 0)),
            whole,
            whole,
            pl.BlockSpec((levels, part_y), lambda i: (0, 0)),
            anywhere,
        ],
        out_specs=[whole, pl.BlockSpec((sublanes, levels, part_y), lambda i: (i, 0, 0))],
        out_shape=[
            jax.ShapeDtypeStruct(base.shape, jnp.float32),
            jax.ShapeDtypeStruct(base.shape[1:], jnp.float32),
        ],
        input_output_aliases={3: 0},
        name="gradient_of",
        **parameters(6 * size * levels, 7 * size, 2 * size),
    )(rows, wide(matrix[None]), base, done, laplace, profile, follow)


def shifted(cells, axis, shift):
    count = lax.axis_size(axis)
    return lax.ppermute(cells, axis, [(i, (i + shift) % count) for i in range(count)])


def swap_x(rows):
    return lax.all_to_all(rows, "gx", split_axis=0, concat_axis=0, tiled=True)


def gate_kernel(*refs):
    del refs


def gate(pieces, before, weight=0):
    count = len(pieces)
    return pl.pallas_call(
        gate_kernel,
        in_specs=[anywhere] * (count + len(before)),
        out_specs=[anywhere] * count,
        out_shape=[jax.ShapeDtypeStruct(p.shape, p.dtype) for p in pieces],
        input_output_aliases={i: i for i in range(count)},
        cost_estimate=pl.CostEstimate(
            flops=0, bytes_accessed=weight * pieces[0].size, transcendentals=0
        ),
        name="gate",
    )(*pieces, *before)


def swap_y(pieces, before, weight=0):
    own, *sent = pieces
    if before:
        sent = gate(sent, before, weight)
    return [own] + [shifted(piece, "gy", s) for s, piece in enumerate(sent, 1)]


def matmul(a, b):
    return jnp.dot(a, b, precision=precise)


def body(
    velocity,
    cotangent,
    coefficient,
    level_profile,
    vert_deriv,
    eigen_vectors,
    eigen_inverse,
    eigen_rates,
):
    count_x = lax.axis_size("gx")
    count_y = lax.axis_size("gy")
    full_x = count_x * velocity.shape[1]
    full_y = count_y * velocity.shape[3]
    per = velocity.shape[2] // count_x
    me = lax.axis_index("gy").astype(jnp.int32).reshape(1)
    rates = lax.dynamic_slice_in_dim(eigen_rates, lax.axis_index("gx") * per, per)

    forward, forward_slope, inverse, inverse_slope = line_transform(full_x)
    plain_x = grouped(forward, count_y)
    joint_x = np.concatenate([grouped(forward_slope, count_y), plain_x], axis=2)
    table_plain, table_joint = halves(plain_x), halves(joint_x)

    def columns(*tables):
        turned = [np.swapaxes(grouped(table, count_y), 1, 2) for table in tables]
        return halves(np.stack(turned))

    back_plain, back_joint = columns(inverse), columns(inverse_slope, inverse)

    forward, forward_slope, inverse, inverse_slope = line_transform(full_y)

    def points(table):
        return table.reshape(full_y, count_y, full_y // count_y).transpose(1, 2, 0)

    y_forward = halves(np.stack([points(forward), points(forward_slope)]))
    y_inverse = halves(
        np.stack([np.swapaxes(points(table), 1, 2) for table in (inverse, inverse_slope)])
    )

    vectors_t = eigen_vectors.T
    inverse_t = eigen_inverse.T
    deriv_t = vert_deriv.T

    profile = jnp.broadcast_to(level_profile[:, None], velocity.shape[2:])

    a_one = into_levels(cotangent, -vectors_t[None], (1,), count_x)
    last = matmul(vectors_t, deriv_t)
    a_two = into_levels(cotangent, jnp.stack([-vectors_t, last]), (0, 2), count_x, a_one)
    low, high, first, final = edges_of(velocity, a_one)
    sides = (shifted(final, "gx", 1), shifted(first, "gx", -1))
    lanes = -(-velocity.shape[1] // 128) * 128
    edges = [
        jnp.pad(edge, ((0, 0), (0, 0), (0, lanes - edge.shape[2])))
        for edge in (shifted(high, "gy", 1), shifted(low, "gy", -1))
    ]
    a_one = swap_x(a_one)
    a_sloped = x_forward(me, a_one, table_plain, *sides, *edges)
    a_two = swap_x(*gate([a_two], [a_one]))
    last = matmul(eigen_inverse, vert_deriv)
    common = (velocity, sides, edges, coefficient, profile, vert_deriv)
    section, laplace, f_one = make_section(
        *common, eigen_inverse[None], count_x, (1,), (), (a_sloped[0],)
    )
    section, laplace, f_two = make_section(
        *common, jnp.stack([eigen_inverse, last]), count_x, (0, 2), (section, laplace), ()
    )
    a_sloped = swap_y(a_sloped, ())
    a_plain = x_forward(me, a_two, table_joint, f_two)
    f_one = swap_x(*gate([f_one], [a_plain[0], *a_sloped]))
    a_plain = swap_y(a_plain, a_sloped)
    f_sloped = x_forward(me, f_one, table_plain, *a_sloped)
    f_two = swap_x(*gate([f_two], [f_sloped[0]]))
    f_sloped = swap_y(f_sloped, a_plain)
    def solve(plain, sloped, follow):
        full = (full_x, full_y)
        return y_solve(plain, sloped, rates, me, y_forward, y_inverse, full, follow)

    a_flat, a_bent = solve(a_plain, a_sloped, f_sloped[0])
    a_flat = swap_y(a_flat, f_sloped)
    f_plain = x_forward(me, f_two, table_joint, *f_sloped)
    f_plain = swap_y(f_plain, a_flat)
    a_two = x_inverse(me, a_flat, back_joint, count_x, f_plain[0])
    a_bent = swap_y(a_bent, (*f_plain, a_two))
    a_two = swap_x(a_two)
    f_flat, f_bent = solve(f_plain, f_sloped, a_bent[0])
    f_flat = swap_y(f_flat, a_bent)
    a_one = x_inverse(me, a_bent, back_plain, count_x, f_flat[0])
    last = -matmul(deriv_t, inverse_t)
    adjoint = from_levels(a_two, jnp.stack([inverse_t, last]), cotangent, (0, 2), False)
    f_bent = swap_y(f_bent, (*f_flat, adjoint))
    a_one = swap_x(*gate([a_one], [a_two]))
    f_two = x_inverse(me, f_flat, back_joint, count_x, a_one)
    f_one = x_inverse(me, f_bent, back_plain, count_x, f_two)
    f_two = swap_x(f_two)
    f_one = swap_x(*gate([f_one], [f_two]))

    adjoint_velocity, gradient = gradient_of(
        a_one, inverse_t, cotangent, adjoint, laplace, profile, f_bent[1]
    )
    last = -matmul(vert_deriv, eigen_vectors)
    new_velocity = from_levels(
        f_two, jnp.stack([-eigen_vectors, last]), section, (0, 2), True
    )
    new_velocity = from_levels(f_one, -eigen_vectors[None], new_velocity, (1,), True)
    return (new_velocity, adjoint_velocity, gradient)


def solution(mesh):
    in_specs = (
        P(None, "gx", None, "gy"),
        P(None, "gx", None, "gy"),
        P("gx", None, "gy"),
        P(),
        P(),
        P(),
        P(),
        P(),
    )
    out_specs = (P(None, "gx", None, "gy"), P(None, "gx", None, "gy"), P("gx", None, "gy"))
    return jax.shard_map(body, mesh=mesh, in_specs=in_specs, out_specs=out_specs, check_vma=False)
```

```python
import functools
import math

import jax
import jax.numpy as jnp
import numpy as np
from jax import lax
from jax.experimental import pallas as pl
from jax.experimental.pallas import tpu as pltpu
from jax.sharding import PartitionSpec as P

step_weight = 0.3 * 8.0 / 15.0
precise = lax.Precision.HIGHEST
half = jnp.bfloat16
vmem_bytes = 60 * 1024 * 1024


def line_transform(count):
    modes = count // 2
    points = np.arange(count)
    angle = (np.arange(modes)[:, None] * points[None, :] % count) * (2.0 * np.pi / count)
    real = np.cos(angle)
    imag = -np.sin(angle)
    imag[0] = np.where(points % 2 == 0, 1.0, -1.0)
    scale = np.full((modes, 1), 2.0 / count)
    scale[0] = 1.0 / count
    wave = (np.arange(modes) * (2.0 * np.pi / count))[:, None]
    forward = np.stack([real, imag])
    forward_slope = np.stack([-wave * imag, wave * real])
    inverse = np.stack([scale * real, scale * imag])
    inverse_slope = np.stack([scale * wave * imag, -scale * wave * real])
    return forward, forward_slope, inverse, inverse_slope


def grouped(table, groups):
    parts, modes, points = table.shape
    split = table.reshape(parts, groups, modes // groups, points)
    return np.swapaxes(split, 0, 1).reshape(groups, parts * modes // groups, points)


def halves(table):
    table = table.astype(np.float32)
    high = table.astype(half)
    low = (table - high.astype(np.float32)).astype(half)
    return np.stack([high, low])


def split(values):
    high = values.astype(half)
    low = (values - high.astype(jnp.float32)).astype(half)
    return high, low


def product(left, right):
    def dot(a, b):
        return jnp.dot(a, b, preferred_element_type=jnp.float32)

    return dot(left[0], right[0]) + (dot(left[0], right[1]) + dot(left[1], right[0]))


def parameters(flops, read, written, weight=100):
    return dict(
        compiler_params=pltpu.CompilerParams(vmem_limit_bytes=vmem_bytes),
        cost_estimate=pl.CostEstimate(
            flops=weight * flops, bytes_accessed=4 * weight * (read + written), transcendentals=0
        ),
    )


def block_x(part_x):
    return 16 if part_x % 16 == 0 else 8


def wide(matrix):
    high = lax.reduce_precision(matrix, exponent_bits=8, mantissa_bits=7)
    low = (matrix - high).astype(half)
    high = high.astype(half)
    return jnp.concatenate([high, high, low], axis=-1)


def narrow_product(matrix, field):
    high, low = split(field)
    return jnp.dot(
        matrix, jnp.concatenate([high, low, high], axis=0), preferred_element_type=jnp.float32
    )


anywhere = pl.BlockSpec(memory_space=pl.ANY)
scalars = pl.BlockSpec(memory_space=pltpu.SMEM)


def into_kernel(field_ref, matrix_ref, *refs):
    out_ref, rows_ref = refs[-2:]
    sublanes, levels, part_y = field_ref.shape[1:]
    for pair in range(0, sublanes, 2):
        fields = jnp.concatenate([field_ref[0, pair], field_ref[0, pair + 1]], axis=1)
        turned = narrow_product(matrix_ref[0], fields)
        for x in (pair, pair + 1):
            rows_ref[pl.ds(x, levels, stride=sublanes), :] = turned[
                :, (x - pair) * part_y : (x - pair + 1) * part_y
            ]
    out_ref[...] = rows_ref[...].reshape(out_ref.shape)


def into_levels(fields, matrices, components, groups, *follow):
    _, part_x, levels, part_y = fields.shape
    sublanes = block_x(part_x)
    count = len(components)
    per = levels // groups
    first, step = components[0], (components[1] - components[0] if count > 1 else 1)
    size = count * part_x * levels * part_y
    return pl.pallas_call(
        into_kernel,
        grid=(count, part_x // sublanes),
        in_specs=[
            pl.BlockSpec(
                (1, sublanes, levels, part_y), lambda f, i: (first + f * step, i, 0, 0)
            ),
            pl.BlockSpec((1, levels, 3 * levels), lambda f, i: (f, 0, 0)),
        ]
        + [anywhere] * len(follow),
        out_specs=pl.BlockSpec((groups, 1, per, sublanes, part_y), lambda f, i: (0, f, 0, i, 0)),
        out_shape=jax.ShapeDtypeStruct((groups, count, per, part_x, part_y), jnp.float32),
        scratch_shapes=[pltpu.VMEM((levels * sublanes, part_y), jnp.float32)],
        name="into_levels",
        **parameters(6 * size * levels, size, size),
    )(fields, matrices, *follow)


def edges_kernel(field_ref, _, low_ref, high_ref, first_ref, last_ref):
    sublanes, levels, part_y = field_ref.shape[1:]
    step = pl.program_id(0)
    lane = lax.broadcasted_iota(jnp.int32, (levels, low_ref.shape[2]), 1)
    for c in range(3):
        low = low_ref[c]
        high = high_ref[c]
        for x in range(sublanes):
            here = lane == step * sublanes + x
            low = jnp.where(here, field_ref[c, x, :, 0:1], low)
            high = jnp.where(here, field_ref[c, x, :, part_y - 1 : part_y], high)
        low_ref[c] = low
        high_ref[c] = high

    @pl.when(step == 0)
    def _():
        first_ref[...] = field_ref[:, 0:1]

    @pl.when(step == pl.num_programs(0) - 1)
    def _():
        last_ref[...] = field_ref[:, sublanes - 1 :]


def edges_of(field, follow):
    _, part_x, levels, part_y = field.shape
    sublanes = block_x(part_x)
    size = part_x * levels * part_y
    shapes = [(3, levels, part_x)] * 2 + [(3, 1, levels, part_y)] * 2
    return pl.pallas_call(
        edges_kernel,
        grid=(part_x // sublanes,),
        in_specs=[
            pl.BlockSpec((3, sublanes, levels, part_y), lambda i: (0, i, 0, 0)),
            anywhere,
        ],
        out_specs=[pl.BlockSpec(shapes[0], lambda i: (0, 0, 0))] * 2
        + [pl.BlockSpec(shapes[2], lambda i: (0, 0, 0, 0))] * 2,
        out_shape=[jax.ShapeDtypeStruct(shape, jnp.float32) for shape in shapes],
        name="edges_of",
        **parameters(0, 3 * size, 0),
    )(field, follow)


def section_kernel(*refs):
    field_ref, own_ref, before_ref, after_ref, west_ref, east_ref, south_ref, north_ref = refs[:8]
    coefficient_ref, profile_ref, deriv_ref, matrix_ref = refs[8:12]
    section_ref, laplace_ref, out_ref, rows_ref = refs[-4:]
    sublanes, levels, part_y = field_ref.shape[1:]
    edges = south_ref.shape[2]
    step = pl.program_id(1)
    last = pl.num_programs(1) - 1
    lane = lax.broadcasted_iota(jnp.int32, (levels, part_y), 1)
    profile = step_weight * profile_ref[...]
    for pair in range(0, sublanes, 2):
        own = jnp.concatenate([own_ref[0, pair], own_ref[0, pair + 1]], axis=1)
        slopes = narrow_product(deriv_ref[...], own)
        sections = []
        for x in (pair, pair + 1):
            place = step * sublanes + x
            field = own_ref[0, x]
            if x == 0:
                west = jnp.where(step == 0, west_ref[0, 0], before_ref[0, 0])
            else:
                west = own_ref[0, x - 1]
            if x == sublanes - 1:
                east = jnp.where(step == last, east_ref[0, 0], after_ref[0, 0])
            else:
                east = own_ref[0, x + 1]
            low = pltpu.roll(south_ref[0], lax.rem(edges - place, edges), 1)[:, :part_y]
            high = pltpu.roll(north_ref[0], lax.rem(edges + part_y - 1 - place, edges), 1)
            south = jnp.where(lane == 0, low, pltpu.roll(field, 1, 1))
            north = jnp.where(
                lane == part_y - 1, high[:, :part_y], pltpu.roll(field, part_y - 1, 1)
            )
            laplace = east + west + north + south - 4.0 * field
            slope_z = slopes[:, (x - pair) * part_y : (x - pair + 1) * part_y]
            advect = (0.5 * field_ref[0, x]) * (east - west)
            advect = advect + (0.5 * field_ref[1, x]) * (north - south)
            advect = advect + field_ref[2, x] * slope_z
            viscosity = profile * coefficient_ref[x]
            section = field + (viscosity * laplace - step_weight * advect)
            laplace_ref[0, x] = laplace
            section_ref[0, x] = section
            sections.append(section)
        turned = narrow_product(matrix_ref[0], jnp.concatenate(sections, axis=1))
        for x in (pair, pair + 1):
            rows_ref[pl.ds(x, levels, stride=sublanes), :] = turned[
                :, (x - pair) * part_y : (x - pair + 1) * part_y
            ]
    out_ref[...] = rows_ref[...].reshape(out_ref.shape)


def make_section(
    field, sides, edges, coefficient, profile, deriv, matrices, groups, components, done, follow
):
    _, part_x, levels, part_y = field.shape
    sublanes = block_x(part_x)
    per = levels // groups
    count = len(components)
    first, step = components[0], (components[1] - components[0] if count > 1 else 1)
    size = count * part_x * levels * part_y
    whole = pl.BlockSpec((3, sublanes, levels, part_y), lambda f, i: (0, i, 0, 0))
    own = pl.BlockSpec((1, sublanes, levels, part_y), lambda f, i: (first + f * step, i, 0, 0))
    plane = (1, 1, levels, part_y)
    fixed = pl.BlockSpec(plane, lambda f, i: (first + f * step, 0, 0, 0))
    edge = pl.BlockSpec((1, *edges[0].shape[1:]), lambda f, i: (first + f * step, 0, 0))
    full = jax.ShapeDtypeStruct(field.shape, jnp.float32)
    return pl.pallas_call(
        section_kernel,
        grid=(count, part_x // sublanes),
        in_specs=[
            whole,
            own,
            pl.BlockSpec(
                plane, lambda f, i: (first + f * step, jnp.maximum(i * sublanes - 1, 0), 0, 0)
            ),
            pl.BlockSpec(
                plane,
                lambda f, i: (
                    first + f * step,
                    jnp.minimum((i + 1) * sublanes, part_x - 1),
                    0,
                    0,
                ),
            ),
            fixed,
            fixed,
            edge,
            edge,
            pl.BlockSpec((sublanes, levels, part_y), lambda f, i: (i, 0, 0)),
            pl.BlockSpec((levels, part_y), lambda f, i: (0, 0)),
            pl.BlockSpec((levels, 3 * levels), lambda f, i: (0, 0)),
            pl.BlockSpec((1, levels, 3 * levels), lambda f, i: (f, 0, 0)),
        ]
        + [anywhere] * (len(done) + len(follow)),
        out_specs=[
            own,
            own,
            pl.BlockSpec((groups, 1, per, sublanes, part_y), lambda f, i: (0, f, 0, i, 0)),
        ],
        out_shape=[
            full,
            full,
            jax.ShapeDtypeStruct((groups, count, per, part_x, part_y), jnp.float32),
        ],
        input_output_aliases={12 + i: i for i in range(len(done))},
        scratch_shapes=[pltpu.VMEM((levels * sublanes, part_y), jnp.float32)],
        name="make_section",
        **parameters(12 * size * levels, 6 * size, 3 * size),
    )(
        field,
        field,
        field,
        field,
        *sides,
        *edges,
        coefficient,
        profile,
        deriv,
        matrices,
        *done,
        *follow,
    )


def x_kernel(me_ref, rows_ref, table_ref, *refs):
    targets = table_ref.shape[1]
    out_refs = refs[-targets:]
    groups, count, block, part_x, part_y = rows_ref.shape
    columns = []
    for m in range(block):
        lines = [rows_ref[:, f, m].reshape(groups * part_x, part_y) for f in range(count)]
        columns.append(jnp.concatenate(lines, axis=0))
    data = split(jnp.concatenate(columns, axis=1))
    order = [lax.rem(me_ref[0] + s, targets) for s in range(targets)]
    spectrum = product(
        [jnp.concatenate([table_ref[h, o] for o in order], axis=0) for h in range(2)], data
    )
    lines = table_ref.shape[2]
    for s, out_ref in enumerate(out_refs):
        for m in range(block):
            out_ref[m] = spectrum[
                s * lines : (s + 1) * lines, m * part_y : (m + 1) * part_y
            ]


def block_of(levels):
    return 2 if levels % 2 == 0 else 1


def x_forward(me, rows, table, *follow):
    groups, count, levels, part_x, part_y = rows.shape
    targets, lines, depth = table.shape[1:]
    block = block_of(levels)
    size = groups * count * levels * part_x * part_y
    return pl.pallas_call(
        x_kernel,
        grid=(levels // block,),
        in_specs=[
            scalars,
            pl.BlockSpec((groups, count, block, part_x, part_y), lambda i: (0, 0, i, 0, 0)),
            pl.BlockSpec(table.shape, lambda i: (0, 0, 0, 0)),
        ]
        + [anywhere] * len(follow),
        out_specs=[pl.BlockSpec((block, lines, part_y), lambda i: (i, 0, 0))] * targets,
        out_shape=[jax.ShapeDtypeStruct((levels, lines, part_y), jnp.float32)] * targets,
        name="x_forward",
        **parameters(6 * size * targets * lines, size + table.size // 2, size // count),
    )(me, rows, table, *follow)


def solve_kernel(sources, full, group_ref, rates_ref, _, *refs):
    full_x, full_y = full
    in_refs = refs[: 2 * sources]
    forward_ref, inverse_ref = refs[2 * sources : 2 * sources + 2]
    out_refs = refs[2 * sources + 2 :]
    block, lines, part_y = in_refs[0].shape
    me = group_ref[0]
    data = split(
        jnp.concatenate([ref[...].reshape(block * lines, part_y) for ref in in_refs], axis=1)
    )
    origins = [lax.rem(me + sources - s, sources) for s in range(sources)]
    diverg = product(
        data,
        [
            jnp.concatenate([forward_ref[h, p, o] for p in range(2) for o in origins], axis=0)
            for h in range(2)
        ],
    )
    shape = (lines, full_y)
    pairs = lines // 2
    mode_x = me * pairs + lax.broadcasted_iota(jnp.int32, shape, 0) % pairs
    mode_y = lax.broadcasted_iota(jnp.int32, shape, 1) % (full_y // 2)
    wave_x = mode_x.astype(jnp.float32) * (2.0 * math.pi / full_x)
    wave_y = mode_y.astype(jnp.float32) * (2.0 * math.pi / full_y)
    squares = wave_x * wave_x + wave_y * wave_y
    solved = []
    for m in range(block):
        rate = rates_ref[pl.program_id(0) * block + m]
        solved.append(-diverg[m * lines : (m + 1) * lines] / (rate + squares))
    solved = split(jnp.concatenate(solved, axis=0))
    for s, out_ref in enumerate(out_refs):
        place = (s // sources, lax.rem(me + s, sources))
        result = product(solved, (inverse_ref[(0, *place)], inverse_ref[(1, *place)]))
        out_ref[...] = result.reshape(block, lines, part_y)


def y_solve(plain, sloped, rates, group, forward, inverse, full, follow):
    levels, lines, part_y = plain[0].shape
    sources = len(plain)
    block = block_of(levels)
    size = levels * lines * part_y * sources
    targets = 2 * sources
    spec = pl.BlockSpec((block, lines, part_y), lambda i: (i, 0, 0))
    fixed = pl.BlockSpec(forward.shape, lambda i: (0, 0, 0, 0, 0))
    outs = pl.pallas_call(
        functools.partial(solve_kernel, sources, full),
        grid=(levels // block,),
        in_specs=[scalars, scalars, anywhere]
        + [spec] * (2 * sources)
        + [fixed, pl.BlockSpec(inverse.shape, lambda i: (0, 0, 0, 0, 0))],
        out_specs=[spec] * targets,
        out_shape=[jax.ShapeDtypeStruct((levels, lines, part_y), jnp.float32)] * targets,
        name="y_solve",
        **parameters(
            24 * size * full[1], 2 * size + forward.size // 2 + inverse.size // 2, 2 * size
        ),
    )(group, rates, follow, *plain, *sloped, forward, inverse)
    return outs[:sources], outs[sources:]


def x_inverse_kernel(sources, me_ref, _, *refs):
    in_refs = refs[:sources]
    table_ref, out_ref, high_ref, low_ref, rows_ref = refs[sources:]
    _, _, part_x, levels, part_y = out_ref.shape

    @pl.when((pl.program_id(0) == 0) & (pl.program_id(1) == 0))
    def _():
        for m in range(levels):
            high, low = split(jnp.concatenate([ref[m] for ref in in_refs], axis=0))
            high_ref[:, m * part_y : (m + 1) * part_y] = high
            low_ref[:, m * part_y : (m + 1) * part_y] = low

    origins = [lax.rem(me_ref[0] + sources - s, sources) for s in range(sources)]
    table = [
        jnp.concatenate([table_ref[h, 0, o] for o in origins], axis=1) for h in range(2)
    ]
    lines = table[0].shape[0]
    block = block_of(levels)
    for start in range(0, levels, block):
        cut = slice(start * part_y, (start + block) * part_y)
        result = product(table, (high_ref[:, cut], low_ref[:, cut]))
        for m in range(block):
            rows_ref[pl.ds(start + m, lines, stride=levels), :] = result[
                :, m * part_y : (m + 1) * part_y
            ]
    out_ref[...] = rows_ref[...].reshape(out_ref.shape)


def x_inverse(me, pieces, table, groups, follow, weight=100):
    sources = len(pieces)
    levels, lines, part_y = pieces[0].shape
    count, full_x = table.shape[1], table.shape[3]
    part_x = full_x // groups
    steps = 2 if groups % 2 == 0 else 1
    rows = full_x // steps
    size = levels * full_x * part_y
    return pl.pallas_call(
        functools.partial(x_inverse_kernel, sources),
        grid=(count, steps),
        in_specs=[scalars, anywhere]
        + [pl.BlockSpec((levels, lines, part_y), lambda f, i: (0, 0, 0))] * sources
        + [pl.BlockSpec((2, 1, sources, rows, lines), lambda f, i: (0, f, 0, i, 0))],
        out_specs=pl.BlockSpec(
            (groups // steps, 1, part_x, levels, part_y), lambda f, i: (i, f, 0, 0, 0)
        ),
        out_shape=jax.ShapeDtypeStruct((groups, count, part_x, levels, part_y), jnp.float32),
        scratch_shapes=[pltpu.VMEM((full_x, levels * part_y), half)] * 2
        + [pltpu.VMEM((rows * levels, part_y), jnp.float32)],
        name="x_inverse",
        **parameters(
            6 * size * full_x * count, size + table.size // 2, size * count, weight
        ),
    )(me, follow, *pieces, table)


def column(rows_ref, component, x):
    groups = rows_ref.shape[0]
    return jnp.concatenate([rows_ref[g, component, x] for g in range(groups)], axis=0)


def from_kernel(rows_ref, matrix_ref, base_ref, *refs):
    out_ref = refs[-1]
    part_y = base_ref.shape[3]
    for pair in range(0, base_ref.shape[1], 2):
        fields = [column(rows_ref, 0, x) for x in (pair, pair + 1)]
        turned = narrow_product(matrix_ref[0], jnp.concatenate(fields, axis=1))
        out_ref[0, pair] = base_ref[0, pair] + turned[:, :part_y]
        out_ref[0, pair + 1] = base_ref[0, pair + 1] + turned[:, part_y:]


def from_levels(rows, matrices, base, components, in_place, *follow):
    groups, count, part_x, per, part_y = rows.shape
    levels = groups * per
    sublanes = block_x(part_x)
    first, step = components[0], (components[1] - components[0] if count > 1 else 1)
    size = count * part_x * levels * part_y
    spec = pl.BlockSpec((1, sublanes, levels, part_y), lambda f, i: (first + f * step, i, 0, 0))
    return pl.pallas_call(
        from_kernel,
        grid=(count, part_x // sublanes),
        in_specs=[
            pl.BlockSpec((groups, 1, sublanes, per, part_y), lambda f, i: (0, f, i, 0, 0)),
            pl.BlockSpec((1, levels, 3 * levels), lambda f, i: (f, 0, 0)),
            spec,
        ]
        + [anywhere] * len(follow),
        out_specs=spec,
        out_shape=jax.ShapeDtypeStruct(base.shape, jnp.float32),
        input_output_aliases={2: 0} if in_place else {},
        name="from_levels",
        **parameters(6 * size * levels, 2 * size, size),
    )(rows, matrices, base, *follow)


def gradient_kernel(
    rows_ref, matrix_ref, base_ref, done_ref, laplace_ref, profile_ref, _, out_ref, gradient_ref
):
    profile = step_weight * profile_ref[...]
    part_y = base_ref.shape[3]
    for pair in range(0, base_ref.shape[1], 2):
        fields = [column(rows_ref, 0, x) for x in (pair, pair + 1)]
        turned = narrow_product(matrix_ref[0], jnp.concatenate(fields, axis=1))
        for x in (pair, pair + 1):
            value = base_ref[0, x] + turned[:, (x - pair) * part_y : (x - pair + 1) * part_y]
            first, last = done_ref[0, x], done_ref[2, x]
            out_ref[0, x], out_ref[1, x], out_ref[2, x] = first, value, last
            total = first * laplace_ref[0, x] + value * laplace_ref[1, x]
            gradient_ref[x] = profile * (total + last * laplace_ref[2, x])


def gradient_of(rows, matrix, base, done, laplace, profile, follow):
    groups, _, part_x, per, part_y = rows.shape
    levels = groups * per
    sublanes = block_x(part_x)
    size = part_x * levels * part_y

    whole = pl.BlockSpec((3, sublanes, levels, part_y), lambda i: (0, i, 0, 0))
    return pl.pallas_call(
        gradient_kernel,
        grid=(part_x // sublanes,),
        in_specs=[
            pl.BlockSpec((groups, 1, sublanes, per, part_y), lambda i: (0, 0, i, 0, 0)),
            pl.BlockSpec((1, levels, 3 * levels), lambda i: (0, 0, 0)),
            pl.BlockSpec((1, sublanes, levels, part_y), lambda i: (1, i, 0, 0)),
            whole,
            whole,
            pl.BlockSpec((levels, part_y), lambda i: (0, 0)),
            anywhere,
        ],
        out_specs=[whole, pl.BlockSpec((sublanes, levels, part_y), lambda i: (i, 0, 0))],
        out_shape=[
            jax.ShapeDtypeStruct(base.shape, jnp.float32),
            jax.ShapeDtypeStruct(base.shape[1:], jnp.float32),
        ],
        input_output_aliases={3: 0},
        name="gradient_of",
        **parameters(6 * size * levels, 7 * size, 2 * size),
    )(rows, matrix, base, done, laplace, profile, follow)


def shifted(cells, axis, shift):
    count = lax.axis_size(axis)
    return lax.ppermute(cells, axis, [(i, (i + shift) % count) for i in range(count)])


def swap_x(rows):
    return lax.all_to_all(rows, "gx", split_axis=0, concat_axis=0, tiled=True)


def gate_kernel(*refs):
    del refs


def gate(pieces, before, weight=0):
    count = len(pieces)
    return pl.pallas_call(
        gate_kernel,
        in_specs=[anywhere] * (count + len(before)),
        out_specs=[anywhere] * count,
        out_shape=[jax.ShapeDtypeStruct(p.shape, p.dtype) for p in pieces],
        input_output_aliases={i: i for i in range(count)},
        cost_estimate=pl.CostEstimate(
            flops=0, bytes_accessed=weight * pieces[0].size, transcendentals=0
        ),
        name="gate",
    )(*pieces, *before)


def swap_y(pieces, before, weight=0):
    own, *sent = pieces
    if before:
        sent = gate(sent, before, weight)
    return [own] + [shifted(piece, "gy", s) for s, piece in enumerate(sent, 1)]


def matmul(a, b):
    return jnp.dot(a, b, precision=precise)


def body(
    velocity,
    cotangent,
    coefficient,
    level_profile,
    vert_deriv,
    eigen_vectors,
    eigen_inverse,
    eigen_rates,
):
    count_x = lax.axis_size("gx")
    count_y = lax.axis_size("gy")
    full_x = count_x * velocity.shape[1]
    full_y = count_y * velocity.shape[3]
    per = velocity.shape[2] // count_x
    me = lax.axis_index("gy").astype(jnp.int32).reshape(1)
    rates = lax.dynamic_slice_in_dim(eigen_rates, lax.axis_index("gx") * per, per)

    forward, forward_slope, inverse, inverse_slope = line_transform(full_x)
    plain_x = grouped(forward, count_y)
    joint_x = np.concatenate([grouped(forward_slope, count_y), plain_x], axis=2)
    table_plain, table_joint = halves(plain_x), halves(joint_x)

    def columns(*tables):
        turned = [np.swapaxes(grouped(table, count_y), 1, 2) for table in tables]
        return halves(np.stack(turned))

    back_plain, back_joint = columns(inverse), columns(inverse_slope, inverse)

    forward, forward_slope, inverse, inverse_slope = line_transform(full_y)

    def points(table):
        return table.reshape(full_y, count_y, full_y // count_y).transpose(1, 2, 0)

    y_forward = halves(np.stack([points(forward), points(forward_slope)]))
    y_inverse = halves(
        np.stack([np.swapaxes(points(table), 1, 2) for table in (inverse, inverse_slope)])
    )

    vectors_t = eigen_vectors.T
    inverse_t = eigen_inverse.T
    deriv_t = vert_deriv.T
    profile = jnp.broadcast_to(level_profile[:, None], velocity.shape[2:])
    enter_adjoint = wide(jnp.stack([-vectors_t, matmul(vectors_t, deriv_t)]))
    enter_forward = wide(jnp.stack([eigen_inverse, matmul(eigen_inverse, vert_deriv)]))
    leave_adjoint = wide(jnp.stack([inverse_t, -matmul(deriv_t, inverse_t)]))
    leave_forward = wide(-jnp.stack([eigen_vectors, matmul(vert_deriv, eigen_vectors)]))
    slope = wide(vert_deriv)

    a_one = into_levels(cotangent, wide(-vectors_t[None]), (1,), count_x)
    a_two = into_levels(
        cotangent,
        enter_adjoint,
        (0, 2),
        count_x,
        a_one,
        enter_forward,
        leave_adjoint,
        leave_forward,
        slope,
        profile,
    )
    low, high, first, final = edges_of(velocity, a_one)
    sides = (shifted(final, "gx", 1), shifted(first, "gx", -1))
    lanes = -(-velocity.shape[1] // 128) * 128
    edges = [
        jnp.pad(edge, ((0, 0), (0, 0), (0, lanes - edge.shape[2])))
        for edge in (shifted(high, "gy", 1), shifted(low, "gy", -1))
    ]
    a_one = swap_x(a_one)
    a_sloped = x_forward(me, a_one, table_plain, *sides, *edges)
    a_two = swap_x(*gate([a_two], [a_one]))
    common = (velocity, sides, edges, coefficient, profile, slope)
    section, laplace, f_one = make_section(
        *common, enter_forward, count_x, (1,), (), (a_sloped[0],)
    )
    section, laplace, f_two = make_section(
        *common, enter_forward, count_x, (0, 2), (section, laplace), ()
    )
    a_sloped = swap_y(a_sloped, ())
    a_plain = x_forward(me, a_two, table_joint, f_two)
    f_one = swap_x(*gate([f_one], [a_plain[0], *a_sloped]))
    a_plain = swap_y(a_plain, a_sloped)
    f_sloped = x_forward(me, f_one, table_plain, *a_sloped)
    f_two = swap_x(*gate([f_two], [f_one]))
    f_sloped = swap_y(f_sloped, a_plain)
    f_plain = x_forward(me, f_two, table_joint, *a_plain)

    def solve(plain, sloped, follow):
        full = (full_x, full_y)
        return y_solve(plain, sloped, rates, me, y_forward, y_inverse, full, follow)

    a_flat, a_bent = solve(a_plain, a_sloped, f_plain[0])
    f_plain = swap_y(f_plain, f_sloped)
    a_flat = swap_y(a_flat, f_plain)
    f_flat, f_bent = solve(f_plain, f_sloped, a_bent[0])
    f_flat = swap_y(f_flat, a_flat)
    a_two = x_inverse(me, a_flat, back_joint, count_x, f_flat[0])
    a_bent = swap_y(a_bent, (*f_flat, a_two))
    a_two = swap_x(a_two)
    f_two = x_inverse(me, f_flat, back_joint, count_x, a_bent[0])
    adjoint = from_levels(a_two, leave_adjoint, cotangent, (0, 2), False)
    f_bent = swap_y(f_bent, (*a_bent, adjoint))
    f_two = swap_x(*gate([f_two], [a_two]))
    a_one = x_inverse(me, a_bent, back_plain, count_x, f_bent[0], 10)
    (a_one,) = gate([a_one], [f_two])
    f_one = x_inverse(me, f_bent, back_plain, count_x, a_one)
    a_one = swap_x(a_one)
    f_one = swap_x(*gate([f_one], [a_one]))

    adjoint_velocity, gradient = gradient_of(
        a_one, leave_adjoint, cotangent, adjoint, laplace, profile, f_bent[1]
    )
    new_velocity = from_levels(f_two, leave_forward, section, (0, 2), True, a_one)
    new_velocity = from_levels(f_one, leave_forward, new_velocity, (1,), True)
    return (new_velocity, adjoint_velocity, gradient)


def solution(mesh):
    in_specs = (
        P(None, "gx", None, "gy"),
        P(None, "gx", None, "gy"),
        P("gx", None, "gy"),
        P(),
        P(),
        P(),
        P(),
        P(),
    )
    out_specs = (P(None, "gx", None, "gy"), P(None, "gx", None, "gy"), P("gx", None, "gy"))
    return jax.shard_map(body, mesh=mesh, in_specs=in_specs, out_specs=out_specs, check_vma=False)
```

```python
import functools
import math

import jax
import jax.numpy as jnp
import numpy as np
from jax import lax
from jax.experimental import pallas as pl
from jax.experimental.pallas import tpu as pltpu
from jax.sharding import PartitionSpec as P

step_weight = 0.3 * 8.0 / 15.0
precise = lax.Precision.HIGHEST
half = jnp.bfloat16
vmem_bytes = 60 * 1024 * 1024


def line_transform(count):
    modes = count // 2
    points = np.arange(count)
    angle = (np.arange(modes)[:, None] * points[None, :] % count) * (2.0 * np.pi / count)
    real = np.cos(angle)
    imag = -np.sin(angle)
    imag[0] = np.where(points % 2 == 0, 1.0, -1.0)
    scale = np.full((modes, 1), 2.0 / count)
    scale[0] = 1.0 / count
    wave = (np.arange(modes) * (2.0 * np.pi / count))[:, None]
    forward = np.stack([real, imag])
    forward_slope = np.stack([-wave * imag, wave * real])
    inverse = np.stack([scale * real, scale * imag])
    inverse_slope = np.stack([scale * wave * imag, -scale * wave * real])
    return forward, forward_slope, inverse, inverse_slope


def grouped(table, groups):
    parts, modes, points = table.shape
    split = table.reshape(parts, groups, modes // groups, points)
    return np.swapaxes(split, 0, 1).reshape(groups, parts * modes // groups, points)


def halves(table):
    table = table.astype(np.float32)
    high = table.astype(half)
    low = (table - high.astype(np.float32)).astype(half)
    return np.stack([high, low])


def split(values):
    high = values.astype(half)
    low = (values - high.astype(jnp.float32)).astype(half)
    return high, low


def product(left, right):
    def dot(a, b):
        return jnp.dot(a, b, preferred_element_type=jnp.float32)

    return dot(left[0], right[0]) + (dot(left[0], right[1]) + dot(left[1], right[0]))


def parameters(flops, read, written, weight=100):
    return dict(
        compiler_params=pltpu.CompilerParams(vmem_limit_bytes=vmem_bytes),
        cost_estimate=pl.CostEstimate(
            flops=weight * flops, bytes_accessed=4 * weight * (read + written), transcendentals=0
        ),
    )


def block_x(part_x):
    return 16 if part_x % 16 == 0 else 8


def wide(matrix):
    high = lax.reduce_precision(matrix, exponent_bits=8, mantissa_bits=7)
    low = (matrix - high).astype(half)
    high = high.astype(half)
    return jnp.concatenate([high, high, low], axis=-1)


def narrow_product(matrix, field):
    high, low = split(field)
    return jnp.dot(
        matrix, jnp.concatenate([high, low, high], axis=0), preferred_element_type=jnp.float32
    )


anywhere = pl.BlockSpec(memory_space=pl.ANY)
scalars = pl.BlockSpec(memory_space=pltpu.SMEM)


def into_kernel(field_ref, matrix_ref, *refs):
    out_ref, rows_ref = refs[-2:]
    sublanes, levels, part_y = field_ref.shape[1:]
    for pair in range(0, sublanes, 2):
        fields = jnp.concatenate([field_ref[0, pair], field_ref[0, pair + 1]], axis=1)
        turned = narrow_product(matrix_ref[0], fields)
        for x in (pair, pair + 1):
            rows_ref[pl.ds(x, levels, stride=sublanes), :] = turned[
                :, (x - pair) * part_y : (x - pair + 1) * part_y
            ]
    out_ref[...] = rows_ref[...].reshape(out_ref.shape)


def into_levels(fields, matrices, components, groups, *follow):
    _, part_x, levels, part_y = fields.shape
    sublanes = block_x(part_x)
    count = len(components)
    per = levels // groups
    first, step = components[0], (components[1] - components[0] if count > 1 else 1)
    size = count * part_x * levels * part_y
    return pl.pallas_call(
        into_kernel,
        grid=(count, part_x // sublanes),
        in_specs=[
            pl.BlockSpec(
                (1, sublanes, levels, part_y), lambda f, i: (first + f * step, i, 0, 0)
            ),
            pl.BlockSpec((1, levels, 3 * levels), lambda f, i: (f, 0, 0)),
        ]
        + [anywhere] * len(follow),
        out_specs=pl.BlockSpec((groups, 1, per, sublanes, part_y), lambda f, i: (0, f, 0, i, 0)),
        out_shape=jax.ShapeDtypeStruct((groups, count, per, part_x, part_y), jnp.float32),
        scratch_shapes=[pltpu.VMEM((levels * sublanes, part_y), jnp.float32)],
        name="into_levels",
        **parameters(6 * size * levels, size, size),
    )(fields, matrices, *follow)


def edges_kernel(field_ref, _, low_ref, high_ref, first_ref, last_ref):
    sublanes, levels, part_y = field_ref.shape[1:]
    step = pl.program_id(0)
    lane = lax.broadcasted_iota(jnp.int32, (levels, low_ref.shape[2]), 1)
    for c in range(3):
        low = low_ref[c]
        high = high_ref[c]
        for x in range(sublanes):
            here = lane == step * sublanes + x
            low = jnp.where(here, field_ref[c, x, :, 0:1], low)
            high = jnp.where(here, field_ref[c, x, :, part_y - 1 : part_y], high)
        low_ref[c] = low
        high_ref[c] = high

    @pl.when(step == 0)
    def _():
        first_ref[...] = field_ref[:, 0:1]

    @pl.when(step == pl.num_programs(0) - 1)
    def _():
        last_ref[...] = field_ref[:, sublanes - 1 :]


def edges_of(field, follow):
    _, part_x, levels, part_y = field.shape
    sublanes = block_x(part_x)
    size = part_x * levels * part_y
    shapes = [(3, levels, part_x)] * 2 + [(3, 1, levels, part_y)] * 2
    return pl.pallas_call(
        edges_kernel,
        grid=(part_x // sublanes,),
        in_specs=[
            pl.BlockSpec((3, sublanes, levels, part_y), lambda i: (0, i, 0, 0)),
            anywhere,
        ],
        out_specs=[pl.BlockSpec(shapes[0], lambda i: (0, 0, 0))] * 2
        + [pl.BlockSpec(shapes[2], lambda i: (0, 0, 0, 0))] * 2,
        out_shape=[jax.ShapeDtypeStruct(shape, jnp.float32) for shape in shapes],
        name="edges_of",
        **parameters(0, 3 * size, 0),
    )(field, follow)


def section_kernel(*refs):
    field_ref, own_ref, before_ref, after_ref, west_ref, east_ref, south_ref, north_ref = refs[:8]
    coefficient_ref, profile_ref, deriv_ref, matrix_ref = refs[8:12]
    section_ref, laplace_ref, out_ref, rows_ref = refs[-4:]
    sublanes, levels, part_y = field_ref.shape[1:]
    edges = south_ref.shape[2]
    step = pl.program_id(1)
    last = pl.num_programs(1) - 1
    lane = lax.broadcasted_iota(jnp.int32, (levels, part_y), 1)
    profile = step_weight * profile_ref[...]
    for pair in range(0, sublanes, 2):
        own = jnp.concatenate([own_ref[0, pair], own_ref[0, pair + 1]], axis=1)
        slopes = narrow_product(deriv_ref[...], own)
        sections = []
        for x in (pair, pair + 1):
            place = step * sublanes + x
            field = own_ref[0, x]
            if x == 0:
                west = jnp.where(step == 0, west_ref[0, 0], before_ref[0, 0])
            else:
                west = own_ref[0, x - 1]
            if x == sublanes - 1:
                east = jnp.where(step == last, east_ref[0, 0], after_ref[0, 0])
            else:
                east = own_ref[0, x + 1]
            low = pltpu.roll(south_ref[0], lax.rem(edges - place, edges), 1)[:, :part_y]
            high = pltpu.roll(north_ref[0], lax.rem(edges + part_y - 1 - place, edges), 1)
            south = jnp.where(lane == 0, low, pltpu.roll(field, 1, 1))
            north = jnp.where(
                lane == part_y - 1, high[:, :part_y], pltpu.roll(field, part_y - 1, 1)
            )
            laplace = east + west + north + south - 4.0 * field
            slope_z = slopes[:, (x - pair) * part_y : (x - pair + 1) * part_y]
            advect = (0.5 * field_ref[0, x]) * (east - west)
            advect = advect + (0.5 * field_ref[1, x]) * (north - south)
            advect = advect + field_ref[2, x] * slope_z
            viscosity = profile * coefficient_ref[x]
            section = field + (viscosity * laplace - step_weight * advect)
            laplace_ref[0, x] = laplace
            section_ref[0, x] = section
            sections.append(section)
        turned = narrow_product(matrix_ref[0], jnp.concatenate(sections, axis=1))
        for x in (pair, pair + 1):
            rows_ref[pl.ds(x, levels, stride=sublanes), :] = turned[
                :, (x - pair) * part_y : (x - pair + 1) * part_y
            ]
    out_ref[...] = rows_ref[...].reshape(out_ref.shape)


def make_section(
    field, sides, edges, coefficient, profile, deriv, matrices, groups, components, done, follow
):
    _, part_x, levels, part_y = field.shape
    sublanes = block_x(part_x)
    per = levels // groups
    count = len(components)
    first, step = components[0], (components[1] - components[0] if count > 1 else 1)
    size = count * part_x * levels * part_y
    whole = pl.BlockSpec((3, sublanes, levels, part_y), lambda f, i: (0, i, 0, 0))
    own = pl.BlockSpec((1, sublanes, levels, part_y), lambda f, i: (first + f * step, i, 0, 0))
    plane = (1, 1, levels, part_y)
    fixed = pl.BlockSpec(plane, lambda f, i: (first + f * step, 0, 0, 0))
    edge = pl.BlockSpec((1, *edges[0].shape[1:]), lambda f, i: (first + f * step, 0, 0))
    full = jax.ShapeDtypeStruct(field.shape, jnp.float32)
    return pl.pallas_call(
        section_kernel,
        grid=(count, part_x // sublanes),
        in_specs=[
            whole,
            own,
            pl.BlockSpec(
                plane, lambda f, i: (first + f * step, jnp.maximum(i * sublanes - 1, 0), 0, 0)
            ),
            pl.BlockSpec(
                plane,
                lambda f, i: (
                    first + f * step,
                    jnp.minimum((i + 1) * sublanes, part_x - 1),
                    0,
                    0,
                ),
            ),
            fixed,
            fixed,
            edge,
            edge,
            pl.BlockSpec((sublanes, levels, part_y), lambda f, i: (i, 0, 0)),
            pl.BlockSpec((levels, part_y), lambda f, i: (0, 0)),
            pl.BlockSpec((levels, 3 * levels), lambda f, i: (0, 0)),
            pl.BlockSpec((1, levels, 3 * levels), lambda f, i: (f, 0, 0)),
        ]
        + [anywhere] * (len(done) + len(follow)),
        out_specs=[
            own,
            own,
            pl.BlockSpec((groups, 1, per, sublanes, part_y), lambda f, i: (0, f, 0, i, 0)),
        ],
        out_shape=[
            full,
            full,
            jax.ShapeDtypeStruct((groups, count, per, part_x, part_y), jnp.float32),
        ],
        input_output_aliases={12 + i: i for i in range(len(done))},
        scratch_shapes=[pltpu.VMEM((levels * sublanes, part_y), jnp.float32)],
        name="make_section",
        **parameters(12 * size * levels, 6 * size, 3 * size),
    )(
        field,
        field,
        field,
        field,
        *sides,
        *edges,
        coefficient,
        profile,
        deriv,
        matrices,
        *done,
        *follow,
    )


def x_kernel(me_ref, rows_ref, table_ref, *refs):
    targets = table_ref.shape[1]
    out_refs = refs[-targets:]
    groups, count, block, part_x, part_y = rows_ref.shape
    columns = []
    for m in range(block):
        lines = [rows_ref[:, f, m].reshape(groups * part_x, part_y) for f in range(count)]
        columns.append(jnp.concatenate(lines, axis=0))
    data = split(jnp.concatenate(columns, axis=1))
    order = [lax.rem(me_ref[0] + s, targets) for s in range(targets)]
    spectrum = product(
        [jnp.concatenate([table_ref[h, o] for o in order], axis=0) for h in range(2)], data
    )
    lines = table_ref.shape[2]
    for s, out_ref in enumerate(out_refs):
        for m in range(block):
            out_ref[m] = spectrum[
                s * lines : (s + 1) * lines, m * part_y : (m + 1) * part_y
            ]


def block_of(levels):
    return 2 if levels % 2 == 0 else 1


def x_forward(me, rows, table, *follow):
    groups, count, levels, part_x, part_y = rows.shape
    targets, lines, depth = table.shape[1:]
    block = block_of(levels)
    size = groups * count * levels * part_x * part_y
    return pl.pallas_call(
        x_kernel,
        grid=(levels // block,),
        in_specs=[
            scalars,
            pl.BlockSpec((groups, count, block, part_x, part_y), lambda i: (0, 0, i, 0, 0)),
            pl.BlockSpec(table.shape, lambda i: (0, 0, 0, 0)),
        ]
        + [anywhere] * len(follow),
        out_specs=[pl.BlockSpec((block, lines, part_y), lambda i: (i, 0, 0))] * targets,
        out_shape=[jax.ShapeDtypeStruct((levels, lines, part_y), jnp.float32)] * targets,
        name="x_forward",
        **parameters(6 * size * targets * lines, size + table.size // 2, size // count),
    )(me, rows, table, *follow)


def solve_kernel(sources, full, group_ref, rates_ref, _, *refs):
    full_x, full_y = full
    in_refs = refs[: 2 * sources]
    forward_ref, inverse_ref = refs[2 * sources : 2 * sources + 2]
    out_refs = refs[2 * sources + 2 :]
    block, lines, part_y = in_refs[0].shape
    me = group_ref[0]
    data = split(
        jnp.concatenate([ref[...].reshape(block * lines, part_y) for ref in in_refs], axis=1)
    )
    origins = [lax.rem(me + sources - s, sources) for s in range(sources)]
    diverg = product(
        data,
        [
            jnp.concatenate([forward_ref[h, p, o] for p in range(2) for o in origins], axis=0)
            for h in range(2)
        ],
    )
    shape = (lines, full_y)
    pairs = lines // 2
    mode_x = me * pairs + lax.broadcasted_iota(jnp.int32, shape, 0) % pairs
    mode_y = lax.broadcasted_iota(jnp.int32, shape, 1) % (full_y // 2)
    wave_x = mode_x.astype(jnp.float32) * (2.0 * math.pi / full_x)
    wave_y = mode_y.astype(jnp.float32) * (2.0 * math.pi / full_y)
    squares = wave_x * wave_x + wave_y * wave_y
    solved = []
    for m in range(block):
        rate = rates_ref[pl.program_id(0) * block + m]
        solved.append(-diverg[m * lines : (m + 1) * lines] / (rate + squares))
    solved = split(jnp.concatenate(solved, axis=0))
    for s, out_ref in enumerate(out_refs):
        place = (s // sources, lax.rem(me + s, sources))
        result = product(solved, (inverse_ref[(0, *place)], inverse_ref[(1, *place)]))
        out_ref[...] = result.reshape(block, lines, part_y)


def y_solve(plain, sloped, rates, group, forward, inverse, full, follow):
    levels, lines, part_y = plain[0].shape
    sources = len(plain)
    block = block_of(levels)
    size = levels * lines * part_y * sources
    targets = 2 * sources
    spec = pl.BlockSpec((block, lines, part_y), lambda i: (i, 0, 0))
    fixed = pl.BlockSpec(forward.shape, lambda i: (0, 0, 0, 0, 0))
    outs = pl.pallas_call(
        functools.partial(solve_kernel, sources, full),
        grid=(levels // block,),
        in_specs=[scalars, scalars, anywhere]
        + [spec] * (2 * sources)
        + [fixed, pl.BlockSpec(inverse.shape, lambda i: (0, 0, 0, 0, 0))],
        out_specs=[spec] * targets,
        out_shape=[jax.ShapeDtypeStruct((levels, lines, part_y), jnp.float32)] * targets,
        name="y_solve",
        **parameters(
            24 * size * full[1], 2 * size + forward.size // 2 + inverse.size // 2, 2 * size
        ),
    )(group, rates, follow, *plain, *sloped, forward, inverse)
    return outs[:sources], outs[sources:]


def x_inverse_kernel(sources, me_ref, _, *refs):
    in_refs = refs[:sources]
    table_ref, out_ref, high_ref, low_ref, rows_ref = refs[sources:]
    _, _, part_x, levels, part_y = out_ref.shape

    @pl.when((pl.program_id(0) == 0) & (pl.program_id(1) == 0))
    def _():
        for m in range(levels):
            high, low = split(jnp.concatenate([ref[m] for ref in in_refs], axis=0))
            high_ref[:, m * part_y : (m + 1) * part_y] = high
            low_ref[:, m * part_y : (m + 1) * part_y] = low

    origins = [lax.rem(me_ref[0] + sources - s, sources) for s in range(sources)]
    table = [
        jnp.concatenate([table_ref[h, 0, o] for o in origins], axis=1) for h in range(2)
    ]
    lines = table[0].shape[0]
    block = block_of(levels)
    for start in range(0, levels, block):
        cut = slice(start * part_y, (start + block) * part_y)
        result = product(table, (high_ref[:, cut], low_ref[:, cut]))
        for m in range(block):
            rows_ref[pl.ds(start + m, lines, stride=levels), :] = result[
                :, m * part_y : (m + 1) * part_y
            ]
    out_ref[...] = rows_ref[...].reshape(out_ref.shape)


def x_inverse(me, pieces, table, groups, follow, weight=100):
    sources = len(pieces)
    levels, lines, part_y = pieces[0].shape
    count, full_x = table.shape[1], table.shape[3]
    part_x = full_x // groups
    steps = 2 if groups % 2 == 0 else 1
    rows = full_x // steps
    size = levels * full_x * part_y
    return pl.pallas_call(
        functools.partial(x_inverse_kernel, sources),
        grid=(count, steps),
        in_specs=[scalars, anywhere]
        + [pl.BlockSpec((levels, lines, part_y), lambda f, i: (0, 0, 0))] * sources
        + [pl.BlockSpec((2, 1, sources, rows, lines), lambda f, i: (0, f, 0, i, 0))],
        out_specs=pl.BlockSpec(
            (groups // steps, 1, part_x, levels, part_y), lambda f, i: (i, f, 0, 0, 0)
        ),
        out_shape=jax.ShapeDtypeStruct((groups, count, part_x, levels, part_y), jnp.float32),
        scratch_shapes=[pltpu.VMEM((full_x, levels * part_y), half)] * 2
        + [pltpu.VMEM((rows * levels, part_y), jnp.float32)],
        name="x_inverse",
        **parameters(
            6 * size * full_x * count, size + table.size // 2, size * count, weight
        ),
    )(me, follow, *pieces, table)


def column(rows_ref, component, x):
    groups = rows_ref.shape[0]
    return jnp.concatenate([rows_ref[g, component, x] for g in range(groups)], axis=0)


def from_kernel(rows_ref, matrix_ref, base_ref, *refs):
    out_ref = refs[-1]
    part_y = base_ref.shape[3]
    for pair in range(0, base_ref.shape[1], 2):
        fields = [column(rows_ref, 0, x) for x in (pair, pair + 1)]
        turned = narrow_product(matrix_ref[0], jnp.concatenate(fields, axis=1))
        out_ref[0, pair] = base_ref[0, pair] + turned[:, :part_y]
        out_ref[0, pair + 1] = base_ref[0, pair + 1] + turned[:, part_y:]


def from_levels(rows, matrices, base, components, in_place, *follow):
    groups, count, part_x, per, part_y = rows.shape
    levels = groups * per
    sublanes = block_x(part_x)
    first, step = components[0], (components[1] - components[0] if count > 1 else 1)
    size = count * part_x * levels * part_y
    spec = pl.BlockSpec((1, sublanes, levels, part_y), lambda f, i: (first + f * step, i, 0, 0))
    return pl.pallas_call(
        from_kernel,
        grid=(count, part_x // sublanes),
        in_specs=[
            pl.BlockSpec((groups, 1, sublanes, per, part_y), lambda f, i: (0, f, i, 0, 0)),
            pl.BlockSpec((1, levels, 3 * levels), lambda f, i: (f, 0, 0)),
            spec,
        ]
        + [anywhere] * len(follow),
        out_specs=spec,
        out_shape=jax.ShapeDtypeStruct(base.shape, jnp.float32),
        input_output_aliases={2: 0} if in_place else {},
        name="from_levels",
        **parameters(6 * size * levels, 2 * size, size),
    )(rows, matrices, base, *follow)


def gradient_kernel(
    rows_ref, matrix_ref, base_ref, done_ref, laplace_ref, profile_ref, _, out_ref, gradient_ref
):
    profile = step_weight * profile_ref[...]
    part_y = base_ref.shape[3]
    for pair in range(0, base_ref.shape[1], 2):
        fields = [column(rows_ref, 0, x) for x in (pair, pair + 1)]
        turned = narrow_product(matrix_ref[0], jnp.concatenate(fields, axis=1))
        for x in (pair, pair + 1):
            value = base_ref[0, x] + turned[:, (x - pair) * part_y : (x - pair + 1) * part_y]
            first, last = done_ref[0, x], done_ref[2, x]
            out_ref[0, x], out_ref[1, x], out_ref[2, x] = first, value, last
            total = first * laplace_ref[0, x] + value * laplace_ref[1, x]
            gradient_ref[x] = profile * (total + last * laplace_ref[2, x])


def gradient_of(rows, matrix, base, done, laplace, profile, follow):
    groups, _, part_x, per, part_y = rows.shape
    levels = groups * per
    sublanes = block_x(part_x)
    size = part_x * levels * part_y

    whole = pl.BlockSpec((3, sublanes, levels, part_y), lambda i: (0, i, 0, 0))
    return pl.pallas_call(
        gradient_kernel,
        grid=(part_x // sublanes,),
        in_specs=[
            pl.BlockSpec((groups, 1, sublanes, per, part_y), lambda i: (0, 0, i, 0, 0)),
            pl.BlockSpec((1, levels, 3 * levels), lambda i: (0, 0, 0)),
            pl.BlockSpec((1, sublanes, levels, part_y), lambda i: (1, i, 0, 0)),
            whole,
            whole,
            pl.BlockSpec((levels, part_y), lambda i: (0, 0)),
            anywhere,
        ],
        out_specs=[whole, pl.BlockSpec((sublanes, levels, part_y), lambda i: (i, 0, 0))],
        out_shape=[
            jax.ShapeDtypeStruct(base.shape, jnp.float32),
            jax.ShapeDtypeStruct(base.shape[1:], jnp.float32),
        ],
        input_output_aliases={3: 0},
        name="gradient_of",
        **parameters(6 * size * levels, 7 * size, 2 * size),
    )(rows, matrix, base, done, laplace, profile, follow)


def shifted(cells, axis, shift):
    count = lax.axis_size(axis)
    return lax.ppermute(cells, axis, [(i, (i + shift) % count) for i in range(count)])


def swap_x(rows):
    return lax.all_to_all(rows, "gx", split_axis=0, concat_axis=0, tiled=True)


def gate_kernel(*refs):
    del refs


def gate(pieces, before, weight=0):
    count = len(pieces)
    return pl.pallas_call(
        gate_kernel,
        in_specs=[anywhere] * (count + len(before)),
        out_specs=[anywhere] * count,
        out_shape=[jax.ShapeDtypeStruct(p.shape, p.dtype) for p in pieces],
        input_output_aliases={i: i for i in range(count)},
        cost_estimate=pl.CostEstimate(
            flops=0, bytes_accessed=weight * pieces[0].size, transcendentals=0
        ),
        name="gate",
    )(*pieces, *before)


def swap_y(pieces, last, before=(), early=True):
    own, *sent = pieces
    if last:
        cut = 1 if early else len(sent)
        sent = [
            *gate(sent[:cut], [*last[1 : 1 + cut], *before]),
            *(gate(sent[cut:], last[1 + cut :]) if early else ()),
        ]
    return [own] + [shifted(piece, "gy", s) for s, piece in enumerate(sent, 1)]


def matmul(a, b):
    return jnp.dot(a, b, precision=precise)


def body(
    velocity,
    cotangent,
    coefficient,
    level_profile,
    vert_deriv,
    eigen_vectors,
    eigen_inverse,
    eigen_rates,
):
    count_x = lax.axis_size("gx")
    count_y = lax.axis_size("gy")
    full_x = count_x * velocity.shape[1]
    full_y = count_y * velocity.shape[3]
    per = velocity.shape[2] // count_x
    me = lax.axis_index("gy").astype(jnp.int32).reshape(1)
    rates = lax.dynamic_slice_in_dim(eigen_rates, lax.axis_index("gx") * per, per)

    forward, forward_slope, inverse, inverse_slope = line_transform(full_x)
    plain_x = grouped(forward, count_y)
    joint_x = np.concatenate([grouped(forward_slope, count_y), plain_x], axis=2)
    table_plain, table_joint = halves(plain_x), halves(joint_x)

    def columns(*tables):
        turned = [np.swapaxes(grouped(table, count_y), 1, 2) for table in tables]
        return halves(np.stack(turned))

    back_plain, back_joint = columns(inverse), columns(inverse_slope, inverse)

    forward, forward_slope, inverse, inverse_slope = line_transform(full_y)

    def points(table):
        return table.reshape(full_y, count_y, full_y // count_y).transpose(1, 2, 0)

    y_forward = halves(np.stack([points(forward), points(forward_slope)]))
    y_inverse = halves(
        np.stack([np.swapaxes(points(table), 1, 2) for table in (inverse, inverse_slope)])
    )

    vectors_t = eigen_vectors.T
    inverse_t = eigen_inverse.T
    deriv_t = vert_deriv.T
    profile = jnp.broadcast_to(level_profile[:, None], velocity.shape[2:])
    enter_adjoint = wide(jnp.stack([-vectors_t, matmul(vectors_t, deriv_t)]))
    enter_forward = wide(jnp.stack([eigen_inverse, matmul(eigen_inverse, vert_deriv)]))
    leave_adjoint = wide(jnp.stack([inverse_t, -matmul(deriv_t, inverse_t)]))
    leave_forward = wide(-jnp.stack([eigen_vectors, matmul(vert_deriv, eigen_vectors)]))
    slope = wide(vert_deriv)

    a_one = into_levels(cotangent, wide(-vectors_t[None]), (1,), count_x)
    a_two = into_levels(
        cotangent,
        enter_adjoint,
        (0, 2),
        count_x,
        a_one,
        enter_forward,
        leave_adjoint,
        leave_forward,
        slope,
        profile,
    )
    low, high, first, final = edges_of(velocity, a_one)
    sides = (shifted(final, "gx", 1), shifted(first, "gx", -1))
    lanes = -(-velocity.shape[1] // 128) * 128
    edges = [
        jnp.pad(edge, ((0, 0), (0, 0), (0, lanes - edge.shape[2])))
        for edge in (shifted(high, "gy", 1), shifted(low, "gy", -1))
    ]
    a_one = swap_x(a_one)
    a_sloped = x_forward(me, a_one, table_plain, *sides, *edges)
    a_two = swap_x(*gate([a_two], [a_one]))
    common = (velocity, sides, edges, coefficient, profile, slope)
    section, laplace, f_one = make_section(
        *common, enter_forward, count_x, (1,), (), (a_sloped[0],)
    )
    section, laplace, f_two = make_section(
        *common, enter_forward, count_x, (0, 2), (section, laplace), ()
    )
    a_sloped = swap_y(a_sloped, ())
    a_plain = x_forward(me, a_two, table_joint, f_two)
    f_one = swap_x(*gate([f_one], [a_plain[0], *a_sloped]))
    a_plain = swap_y(a_plain, a_sloped)
    f_sloped = x_forward(me, f_one, table_plain, *a_sloped)
    f_two = swap_x(*gate([f_two], [f_one]))
    f_sloped = swap_y(f_sloped, a_plain)
    f_plain = x_forward(me, f_two, table_joint, *a_plain)

    def solve(plain, sloped, follow):
        full = (full_x, full_y)
        return y_solve(plain, sloped, rates, me, y_forward, y_inverse, full, follow)

    a_flat, a_bent = solve(a_plain, a_sloped, f_plain[0])
    f_plain = swap_y(f_plain, f_sloped)
    a_flat = swap_y(a_flat, f_plain)
    f_flat, f_bent = solve(f_plain, f_sloped, a_bent[0])
    f_flat = swap_y(f_flat, a_flat, early=False)
    a_two = x_inverse(me, a_flat, back_joint, count_x, f_flat[0])
    a_bent = swap_y(a_bent, f_flat, (a_two,), False)
    a_two = swap_x(a_two)
    f_two = x_inverse(me, f_flat, back_joint, count_x, a_bent[0])
    adjoint = from_levels(a_two, leave_adjoint, cotangent, (0, 2), False)
    f_bent = swap_y(f_bent, a_bent, (adjoint,), False)
    f_two = swap_x(*gate([f_two], [a_two]))
    a_one = x_inverse(me, a_bent, back_plain, count_x, f_bent[0], 10)
    (a_one,) = gate([a_one], [f_two])
    f_one = x_inverse(me, f_bent, back_plain, count_x, a_one)
    a_one = swap_x(a_one)
    f_one = swap_x(*gate([f_one], [a_one]))

    adjoint_velocity, gradient = gradient_of(
        a_one, leave_adjoint, cotangent, adjoint, laplace, profile, f_bent[1]
    )
    new_velocity = from_levels(f_two, leave_forward, section, (0, 2), True, a_one)
    new_velocity = from_levels(f_one, leave_forward, new_velocity, (1,), True)
    return (new_velocity, adjoint_velocity, gradient)


def solution(mesh):
    in_specs = (
        P(None, "gx", None, "gy"),
        P(None, "gx", None, "gy"),
        P("gx", None, "gy"),
        P(),
        P(),
        P(),
        P(),
        P(),
    )
    out_specs = (P(None, "gx", None, "gy"), P(None, "gx", None, "gy"), P("gx", None, "gy"))
    return jax.shard_map(body, mesh=mesh, in_specs=in_specs, out_specs=out_specs, check_vma=False)
```

```python
import functools
import math

import jax
import jax.numpy as jnp
import numpy as np
from jax import lax
from jax.experimental import pallas as pl
from jax.experimental.pallas import tpu as pltpu
from jax.sharding import PartitionSpec as P

step_weight = 0.3 * 8.0 / 15.0
precise = lax.Precision.HIGHEST
half = jnp.bfloat16
vmem_bytes = 60 * 1024 * 1024


def line_transform(count):
    modes = count // 2
    points = np.arange(count)
    angle = (np.arange(modes)[:, None] * points[None, :] % count) * (2.0 * np.pi / count)
    real = np.cos(angle)
    imag = -np.sin(angle)
    imag[0] = np.where(points % 2 == 0, 1.0, -1.0)
    scale = np.full((modes, 1), 2.0 / count)
    scale[0] = 1.0 / count
    wave = (np.arange(modes) * (2.0 * np.pi / count))[:, None]
    forward = np.stack([real, imag])
    forward_slope = np.stack([-wave * imag, wave * real])
    inverse = np.stack([scale * real, scale * imag])
    inverse_slope = np.stack([scale * wave * imag, -scale * wave * real])
    return forward, forward_slope, inverse, inverse_slope


def grouped(table, groups):
    parts, modes, points = table.shape
    split = table.reshape(parts, groups, modes // groups, points)
    return np.swapaxes(split, 0, 1).reshape(groups, parts * modes // groups, points)


def halves(table):
    table = table.astype(np.float32)
    high = table.astype(half)
    low = (table - high.astype(np.float32)).astype(half)
    return np.stack([high, low])


def split(values):
    high = values.astype(half)
    low = (values - high.astype(jnp.float32)).astype(half)
    return high, low


def product(left, right):
    def dot(a, b):
        return jnp.dot(a, b, preferred_element_type=jnp.float32)

    return dot(left[0], right[0]) + (dot(left[0], right[1]) + dot(left[1], right[0]))


def parameters(flops, read, written, weight=100):
    return dict(
        compiler_params=pltpu.CompilerParams(vmem_limit_bytes=vmem_bytes),
        cost_estimate=pl.CostEstimate(
            flops=weight * flops, bytes_accessed=4 * weight * (read + written), transcendentals=0
        ),
    )


def block_x(part_x):
    return 16 if part_x % 16 == 0 else 8


def wide(matrix):
    high = lax.reduce_precision(matrix, exponent_bits=8, mantissa_bits=7)
    low = (matrix - high).astype(half)
    high = high.astype(half)
    return jnp.concatenate([high, high, low], axis=-1)


def narrow_product(matrix, field):
    high, low = split(field)
    return jnp.dot(
        matrix, jnp.concatenate([high, low, high], axis=0), preferred_element_type=jnp.float32
    )


anywhere = pl.BlockSpec(memory_space=pl.ANY)
scalars = pl.BlockSpec(memory_space=pltpu.SMEM)


def into_kernel(plain, field_ref, matrix_ref, *refs):
    out_ref, rows_ref = refs[-2:]
    sublanes, levels, part_y = field_ref.shape[1:]
    if plain:
        matrix = -matrix_ref[...]
        high = matrix.astype(half).astype(jnp.float32)
        matrix = jnp.concatenate([high, high, matrix - high], axis=0).T.astype(half)
    else:
        matrix = matrix_ref[0]
    for pair in range(0, sublanes, 2):
        fields = jnp.concatenate([field_ref[0, pair], field_ref[0, pair + 1]], axis=1)
        turned = narrow_product(matrix, fields)
        for x in (pair, pair + 1):
            rows_ref[pl.ds(x, levels, stride=sublanes), :] = turned[
                :, (x - pair) * part_y : (x - pair + 1) * part_y
            ]
    out_ref[...] = rows_ref[...].reshape(out_ref.shape)


def into_levels(fields, matrices, components, groups, *follow):
    _, part_x, levels, part_y = fields.shape
    sublanes = block_x(part_x)
    count = len(components)
    plain = matrices.ndim == 2
    per = levels // groups
    first, step = components[0], (components[1] - components[0] if count > 1 else 1)
    size = count * part_x * levels * part_y
    return pl.pallas_call(
        functools.partial(into_kernel, plain),
        grid=(count, part_x // sublanes),
        in_specs=[
            pl.BlockSpec(
                (1, sublanes, levels, part_y), lambda f, i: (first + f * step, i, 0, 0)
            ),
            pl.BlockSpec((levels, levels), lambda f, i: (0, 0))
            if plain
            else pl.BlockSpec((1, levels, 3 * levels), lambda f, i: (f, 0, 0)),
        ]
        + [anywhere] * len(follow),
        out_specs=pl.BlockSpec((groups, 1, per, sublanes, part_y), lambda f, i: (0, f, 0, i, 0)),
        out_shape=jax.ShapeDtypeStruct((groups, count, per, part_x, part_y), jnp.float32),
        scratch_shapes=[pltpu.VMEM((levels * sublanes, part_y), jnp.float32)],
        name="into_levels",
        **parameters(6 * size * levels, size, size),
    )(fields, matrices, *follow)


def edges_kernel(field_ref, _, low_ref, high_ref, first_ref, last_ref):
    sublanes, levels, part_y = field_ref.shape[1:]
    step = pl.program_id(0)
    lane = lax.broadcasted_iota(jnp.int32, (levels, low_ref.shape[2]), 1)
    for c in range(3):
        low = low_ref[c]
        high = high_ref[c]
        for x in range(sublanes):
            here = lane == step * sublanes + x
            low = jnp.where(here, field_ref[c, x, :, 0:1], low)
            high = jnp.where(here, field_ref[c, x, :, part_y - 1 : part_y], high)
        low_ref[c] = low
        high_ref[c] = high

    @pl.when(step == 0)
    def _():
        first_ref[...] = field_ref[:, 0:1]

    @pl.when(step == pl.num_programs(0) - 1)
    def _():
        last_ref[...] = field_ref[:, sublanes - 1 :]


def edges_of(field, follow):
    _, part_x, levels, part_y = field.shape
    sublanes = block_x(part_x)
    size = part_x * levels * part_y
    shapes = [(3, levels, part_x)] * 2 + [(3, 1, levels, part_y)] * 2
    return pl.pallas_call(
        edges_kernel,
        grid=(part_x // sublanes,),
        in_specs=[
            pl.BlockSpec((3, sublanes, levels, part_y), lambda i: (0, i, 0, 0)),
            anywhere,
        ],
        out_specs=[pl.BlockSpec(shapes[0], lambda i: (0, 0, 0))] * 2
        + [pl.BlockSpec(shapes[2], lambda i: (0, 0, 0, 0))] * 2,
        out_shape=[jax.ShapeDtypeStruct(shape, jnp.float32) for shape in shapes],
        name="edges_of",
        **parameters(0, 3 * size, 0),
    )(field, follow)


def section_kernel(*refs):
    field_ref, own_ref, before_ref, after_ref, west_ref, east_ref, south_ref, north_ref = refs[:8]
    coefficient_ref, profile_ref, deriv_ref, matrix_ref = refs[8:12]
    section_ref, laplace_ref, out_ref, rows_ref = refs[-4:]
    sublanes, levels, part_y = field_ref.shape[1:]
    edges = south_ref.shape[2]
    step = pl.program_id(1)
    last = pl.num_programs(1) - 1
    lane = lax.broadcasted_iota(jnp.int32, (levels, part_y), 1)
    profile = step_weight * profile_ref[...]
    for pair in range(0, sublanes, 2):
        own = jnp.concatenate([own_ref[0, pair], own_ref[0, pair + 1]], axis=1)
        slopes = narrow_product(deriv_ref[...], own)
        sections = []
        for x in (pair, pair + 1):
            place = step * sublanes + x
            field = own_ref[0, x]
            if x == 0:
                west = jnp.where(step == 0, west_ref[0, 0], before_ref[0, 0])
            else:
                west = own_ref[0, x - 1]
            if x == sublanes - 1:
                east = jnp.where(step == last, east_ref[0, 0], after_ref[0, 0])
            else:
                east = own_ref[0, x + 1]
            low = pltpu.roll(south_ref[0], lax.rem(edges - place, edges), 1)[:, :part_y]
            high = pltpu.roll(north_ref[0], lax.rem(edges + part_y - 1 - place, edges), 1)
            south = jnp.where(lane == 0, low, pltpu.roll(field, 1, 1))
            north = jnp.where(
                lane == part_y - 1, high[:, :part_y], pltpu.roll(field, part_y - 1, 1)
            )
            laplace = east + west + north + south - 4.0 * field
            slope_z = slopes[:, (x - pair) * part_y : (x - pair + 1) * part_y]
            advect = (0.5 * field_ref[0, x]) * (east - west)
            advect = advect + (0.5 * field_ref[1, x]) * (north - south)
            advect = advect + field_ref[2, x] * slope_z
            viscosity = profile * coefficient_ref[x]
            section = field + (viscosity * laplace - step_weight * advect)
            laplace_ref[0, x] = laplace
            section_ref[0, x] = section
            sections.append(section)
        turned = narrow_product(matrix_ref[0], jnp.concatenate(sections, axis=1))
        for x in (pair, pair + 1):
            rows_ref[pl.ds(x, levels, stride=sublanes), :] = turned[
                :, (x - pair) * part_y : (x - pair + 1) * part_y
            ]
    out_ref[...] = rows_ref[...].reshape(out_ref.shape)


def make_section(
    field, sides, edges, coefficient, profile, deriv, matrices, groups, components, done, follow
):
    _, part_x, levels, part_y = field.shape
    sublanes = block_x(part_x)
    per = levels // groups
    count = len(components)
    first, step = components[0], (components[1] - components[0] if count > 1 else 1)
    size = count * part_x * levels * part_y
    whole = pl.BlockSpec((3, sublanes, levels, part_y), lambda f, i: (0, i, 0, 0))
    own = pl.BlockSpec((1, sublanes, levels, part_y), lambda f, i: (first + f * step, i, 0, 0))
    plane = (1, 1, levels, part_y)
    fixed = pl.BlockSpec(plane, lambda f, i: (first + f * step, 0, 0, 0))
    edge = pl.BlockSpec((1, *edges[0].shape[1:]), lambda f, i: (first + f * step, 0, 0))
    full = jax.ShapeDtypeStruct(field.shape, jnp.float32)
    return pl.pallas_call(
        section_kernel,
        grid=(count, part_x // sublanes),
        in_specs=[
            whole,
            own,
            pl.BlockSpec(
                plane, lambda f, i: (first + f * step, jnp.maximum(i * sublanes - 1, 0), 0, 0)
            ),
            pl.BlockSpec(
                plane,
                lambda f, i: (
                    first + f * step,
                    jnp.minimum((i + 1) * sublanes, part_x - 1),
                    0,
                    0,
                ),
            ),
            fixed,
            fixed,
            edge,
            edge,
            pl.BlockSpec((sublanes, levels, part_y), lambda f, i: (i, 0, 0)),
            pl.BlockSpec((levels, part_y), lambda f, i: (0, 0)),
            pl.BlockSpec((levels, 3 * levels), lambda f, i: (0, 0)),
            pl.BlockSpec((1, levels, 3 * levels), lambda f, i: (f, 0, 0)),
        ]
        + [anywhere] * (len(done) + len(follow)),
        out_specs=[
            own,
            own,
            pl.BlockSpec((groups, 1, per, sublanes, part_y), lambda f, i: (0, f, 0, i, 0)),
        ],
        out_shape=[
            full,
            full,
            jax.ShapeDtypeStruct((groups, count, per, part_x, part_y), jnp.float32),
        ],
        input_output_aliases={12 + i: i for i in range(len(done))},
        scratch_shapes=[pltpu.VMEM((levels * sublanes, part_y), jnp.float32)],
        name="make_section",
        **parameters(12 * size * levels, 6 * size, 3 * size),
    )(
        field,
        field,
        field,
        field,
        *sides,
        *edges,
        coefficient,
        profile,
        deriv,
        matrices,
        *done,
        *follow,
    )


def x_kernel(me_ref, rows_ref, table_ref, *refs):
    targets = table_ref.shape[1]
    out_refs = refs[-targets:]
    groups, count, block, part_x, part_y = rows_ref.shape
    columns = []
    for m in range(block):
        lines = [rows_ref[:, f, m].reshape(groups * part_x, part_y) for f in range(count)]
        columns.append(jnp.concatenate(lines, axis=0))
    data = split(jnp.concatenate(columns, axis=1))
    order = [lax.rem(me_ref[0] + s, targets) for s in range(targets)]
    spectrum = product(
        [jnp.concatenate([table_ref[h, o] for o in order], axis=0) for h in range(2)], data
    )
    lines = table_ref.shape[2]
    for s, out_ref in enumerate(out_refs):
        for m in range(block):
            out_ref[m] = spectrum[
                s * lines : (s + 1) * lines, m * part_y : (m + 1) * part_y
            ]


def block_of(levels):
    return 2 if levels % 2 == 0 else 1


def x_forward(me, rows, table, *follow):
    groups, count, levels, part_x, part_y = rows.shape
    targets, lines, depth = table.shape[1:]
    block = block_of(levels)
    size = groups * count * levels * part_x * part_y
    return pl.pallas_call(
        x_kernel,
        grid=(levels // block,),
        in_specs=[
            scalars,
            pl.BlockSpec((groups, count, block, part_x, part_y), lambda i: (0, 0, i, 0, 0)),
            pl.BlockSpec(table.shape, lambda i: (0, 0, 0, 0)),
        ]
        + [anywhere] * len(follow),
        out_specs=[pl.BlockSpec((block, lines, part_y), lambda i: (i, 0, 0))] * targets,
        out_shape=[jax.ShapeDtypeStruct((levels, lines, part_y), jnp.float32)] * targets,
        name="x_forward",
        **parameters(6 * size * targets * lines, size + table.size // 2, size // count),
    )(me, rows, table, *follow)


def solve_kernel(sources, full, group_ref, rates_ref, _, *refs):
    full_x, full_y = full
    in_refs = refs[: 2 * sources]
    forward_ref, inverse_ref = refs[2 * sources : 2 * sources + 2]
    out_refs = refs[2 * sources + 2 :]
    block, lines, part_y = in_refs[0].shape
    me = group_ref[0]
    data = split(
        jnp.concatenate([ref[...].reshape(block * lines, part_y) for ref in in_refs], axis=1)
    )
    origins = [lax.rem(me + sources - s, sources) for s in range(sources)]
    diverg = product(
        data,
        [
            jnp.concatenate([forward_ref[h, p, o] for p in range(2) for o in origins], axis=0)
            for h in range(2)
        ],
    )
    shape = (lines, full_y)
    pairs = lines // 2
    mode_x = me * pairs + lax.broadcasted_iota(jnp.int32, shape, 0) % pairs
    mode_y = lax.broadcasted_iota(jnp.int32, shape, 1) % (full_y // 2)
    wave_x = mode_x.astype(jnp.float32) * (2.0 * math.pi / full_x)
    wave_y = mode_y.astype(jnp.float32) * (2.0 * math.pi / full_y)
    squares = wave_x * wave_x + wave_y * wave_y
    solved = []
    for m in range(block):
        rate = rates_ref[pl.program_id(0) * block + m]
        solved.append(-diverg[m * lines : (m + 1) * lines] / (rate + squares))
    solved = split(jnp.concatenate(solved, axis=0))
    for s, out_ref in enumerate(out_refs):
        place = (s // sources, lax.rem(me + s, sources))
        result = product(solved, (inverse_ref[(0, *place)], inverse_ref[(1, *place)]))
        out_ref[...] = result.reshape(block, lines, part_y)


def y_solve(plain, sloped, rates, group, forward, inverse, full, follow):
    levels, lines, part_y = plain[0].shape
    sources = len(plain)
    block = block_of(levels)
    size = levels * lines * part_y * sources
    targets = 2 * sources
    spec = pl.BlockSpec((block, lines, part_y), lambda i: (i, 0, 0))
    fixed = pl.BlockSpec(forward.shape, lambda i: (0, 0, 0, 0, 0))
    outs = pl.pallas_call(
        functools.partial(solve_kernel, sources, full),
        grid=(levels // block,),
        in_specs=[scalars, scalars, anywhere]
        + [spec] * (2 * sources)
        + [fixed, pl.BlockSpec(inverse.shape, lambda i: (0, 0, 0, 0, 0))],
        out_specs=[spec] * targets,
        out_shape=[jax.ShapeDtypeStruct((levels, lines, part_y), jnp.float32)] * targets,
        name="y_solve",
        **parameters(
            24 * size * full[1], 2 * size + forward.size // 2 + inverse.size // 2, 2 * size
        ),
    )(group, rates, follow, *plain, *sloped, forward, inverse)
    return outs[:sources], outs[sources:]


def x_inverse_kernel(sources, me_ref, _, *refs):
    in_refs = refs[:sources]
    table_ref, out_ref, high_ref, low_ref, rows_ref = refs[sources:]
    _, _, part_x, levels, part_y = out_ref.shape

    @pl.when((pl.program_id(0) == 0) & (pl.program_id(1) == 0))
    def _():
        for m in range(levels):
            high, low = split(jnp.concatenate([ref[m] for ref in in_refs], axis=0))
            high_ref[:, m * part_y : (m + 1) * part_y] = high
            low_ref[:, m * part_y : (m + 1) * part_y] = low

    origins = [lax.rem(me_ref[0] + sources - s, sources) for s in range(sources)]
    table = [
        jnp.concatenate([table_ref[h, 0, o] for o in origins], axis=1) for h in range(2)
    ]
    lines = table[0].shape[0]
    block = block_of(levels)
    for start in range(0, levels, block):
        cut = slice(start * part_y, (start + block) * part_y)
        result = product(table, (high_ref[:, cut], low_ref[:, cut]))
        for m in range(block):
            rows_ref[pl.ds(start + m, lines, stride=levels), :] = result[
                :, m * part_y : (m + 1) * part_y
            ]
    out_ref[...] = rows_ref[...].reshape(out_ref.shape)


def x_inverse(me, pieces, table, groups, follow, weight=100):
    sources = len(pieces)
    levels, lines, part_y = pieces[0].shape
    count, full_x = table.shape[1], table.shape[3]
    part_x = full_x // groups
    steps = 2 if groups % 2 == 0 else 1
    rows = full_x // steps
    size = levels * full_x * part_y
    return pl.pallas_call(
        functools.partial(x_inverse_kernel, sources),
        grid=(count, steps),
        in_specs=[scalars, anywhere]
        + [pl.BlockSpec((levels, lines, part_y), lambda f, i: (0, 0, 0))] * sources
        + [pl.BlockSpec((2, 1, sources, rows, lines), lambda f, i: (0, f, 0, i, 0))],
        out_specs=pl.BlockSpec(
            (groups // steps, 1, part_x, levels, part_y), lambda f, i: (i, f, 0, 0, 0)
        ),
        out_shape=jax.ShapeDtypeStruct((groups, count, part_x, levels, part_y), jnp.float32),
        scratch_shapes=[pltpu.VMEM((full_x, levels * part_y), half)] * 2
        + [pltpu.VMEM((rows * levels, part_y), jnp.float32)],
        name="x_inverse",
        **parameters(
            6 * size * full_x * count, size + table.size // 2, size * count, weight
        ),
    )(me, follow, *pieces, table)


def column(rows_ref, component, x):
    groups = rows_ref.shape[0]
    return jnp.concatenate([rows_ref[g, component, x] for g in range(groups)], axis=0)


def from_kernel(rows_ref, matrix_ref, base_ref, *refs):
    out_ref = refs[-1]
    part_y = base_ref.shape[3]
    for pair in range(0, base_ref.shape[1], 2):
        fields = [column(rows_ref, 0, x) for x in (pair, pair + 1)]
        turned = narrow_product(matrix_ref[0], jnp.concatenate(fields, axis=1))
        out_ref[0, pair] = base_ref[0, pair] + turned[:, :part_y]
        out_ref[0, pair + 1] = base_ref[0, pair + 1] + turned[:, part_y:]


def from_levels(rows, matrices, base, components, in_place, *follow):
    groups, count, part_x, per, part_y = rows.shape
    levels = groups * per
    sublanes = block_x(part_x)
    first, step = components[0], (components[1] - components[0] if count > 1 else 1)
    size = count * part_x * levels * part_y
    spec = pl.BlockSpec((1, sublanes, levels, part_y), lambda f, i: (first + f * step, i, 0, 0))
    return pl.pallas_call(
        from_kernel,
        grid=(count, part_x // sublanes),
        in_specs=[
            pl.BlockSpec((groups, 1, sublanes, per, part_y), lambda f, i: (0, f, i, 0, 0)),
            pl.BlockSpec((1, levels, 3 * levels), lambda f, i: (f, 0, 0)),
            spec,
        ]
        + [anywhere] * len(follow),
        out_specs=spec,
        out_shape=jax.ShapeDtypeStruct(base.shape, jnp.float32),
        input_output_aliases={2: 0} if in_place else {},
        name="from_levels",
        **parameters(6 * size * levels, 2 * size, size),
    )(rows, matrices, base, *follow)


def gradient_kernel(
    rows_ref, matrix_ref, base_ref, done_ref, laplace_ref, profile_ref, _, out_ref, gradient_ref
):
    profile = step_weight * profile_ref[...]
    part_y = base_ref.shape[3]
    for pair in range(0, base_ref.shape[1], 2):
        fields = [column(rows_ref, 0, x) for x in (pair, pair + 1)]
        turned = narrow_product(matrix_ref[0], jnp.concatenate(fields, axis=1))
        for x in (pair, pair + 1):
            value = base_ref[0, x] + turned[:, (x - pair) * part_y : (x - pair + 1) * part_y]
            first, last = done_ref[0, x], done_ref[2, x]
            out_ref[0, x], out_ref[1, x], out_ref[2, x] = first, value, last
            total = first * laplace_ref[0, x] + value * laplace_ref[1, x]
            gradient_ref[x] = profile * (total + last * laplace_ref[2, x])


def gradient_of(rows, matrix, base, done, laplace, profile, follow):
    groups, _, part_x, per, part_y = rows.shape
    levels = groups * per
    sublanes = block_x(part_x)
    size = part_x * levels * part_y

    whole = pl.BlockSpec((3, sublanes, levels, part_y), lambda i: (0, i, 0, 0))
    return pl.pallas_call(
        gradient_kernel,
        grid=(part_x // sublanes,),
        in_specs=[
            pl.BlockSpec((groups, 1, sublanes, per, part_y), lambda i: (0, 0, i, 0, 0)),
            pl.BlockSpec((1, levels, 3 * levels), lambda i: (0, 0, 0)),
            pl.BlockSpec((1, sublanes, levels, part_y), lambda i: (1, i, 0, 0)),
            whole,
            whole,
            pl.BlockSpec((levels, part_y), lambda i: (0, 0)),
            anywhere,
        ],
        out_specs=[whole, pl.BlockSpec((sublanes, levels, part_y), lambda i: (i, 0, 0))],
        out_shape=[
            jax.ShapeDtypeStruct(base.shape, jnp.float32),
            jax.ShapeDtypeStruct(base.shape[1:], jnp.float32),
        ],
        input_output_aliases={3: 0},
        name="gradient_of",
        **parameters(6 * size * levels, 7 * size, 2 * size),
    )(rows, matrix, base, done, laplace, profile, follow)


def shifted(cells, axis, shift):
    count = lax.axis_size(axis)
    return lax.ppermute(cells, axis, [(i, (i + shift) % count) for i in range(count)])


def swap_x(rows):
    return lax.all_to_all(rows, "gx", split_axis=0, concat_axis=0, tiled=True)


def gate_kernel(*refs):
    del refs


def gate(pieces, before, weight=0):
    count = len(pieces)
    return pl.pallas_call(
        gate_kernel,
        in_specs=[anywhere] * (count + len(before)),
        out_specs=[anywhere] * count,
        out_shape=[jax.ShapeDtypeStruct(p.shape, p.dtype) for p in pieces],
        input_output_aliases={i: i for i in range(count)},
        cost_estimate=pl.CostEstimate(
            flops=0, bytes_accessed=weight * pieces[0].size, transcendentals=0
        ),
        name="gate",
    )(*pieces, *before)


def swap_y(pieces, last, before=(), early=True):
    own, *sent = pieces
    if last:
        cut = 1 if early else len(sent)
        sent = [
            *gate(sent[:cut], [*last[1 : 1 + cut], *before]),
            *(gate(sent[cut:], last[1 + cut :]) if early else ()),
        ]
    return [own] + [shifted(piece, "gy", s) for s, piece in enumerate(sent, 1)]


def matmul(a, b):
    return jnp.dot(a, b, precision=precise)


def body(
    velocity,
    cotangent,
    coefficient,
    level_profile,
    vert_deriv,
    eigen_vectors,
    eigen_inverse,
    eigen_rates,
):
    count_x = lax.axis_size("gx")
    count_y = lax.axis_size("gy")
    full_x = count_x * velocity.shape[1]
    full_y = count_y * velocity.shape[3]
    per = velocity.shape[2] // count_x
    me = lax.axis_index("gy").astype(jnp.int32).reshape(1)
    rates = lax.dynamic_slice_in_dim(eigen_rates, lax.axis_index("gx") * per, per)

    forward, forward_slope, inverse, inverse_slope = line_transform(full_x)
    plain_x = grouped(forward, count_y)
    joint_x = np.concatenate([grouped(forward_slope, count_y), plain_x], axis=2)
    table_plain, table_joint = halves(plain_x), halves(joint_x)

    def columns(*tables):
        turned = [np.swapaxes(grouped(table, count_y), 1, 2) for table in tables]
        return halves(np.stack(turned))

    back_plain, back_joint = columns(inverse), columns(inverse_slope, inverse)

    forward, forward_slope, inverse, inverse_slope = line_transform(full_y)

    def points(table):
        return table.reshape(full_y, count_y, full_y // count_y).transpose(1, 2, 0)

    y_forward = halves(np.stack([points(forward), points(forward_slope)]))
    y_inverse = halves(
        np.stack([np.swapaxes(points(table), 1, 2) for table in (inverse, inverse_slope)])
    )

    vectors_t = eigen_vectors.T
    inverse_t = eigen_inverse.T
    deriv_t = vert_deriv.T
    profile = jnp.broadcast_to(level_profile[:, None], velocity.shape[2:])
    enter_adjoint = wide(jnp.stack([-vectors_t, matmul(vectors_t, deriv_t)]))
    enter_forward = wide(jnp.stack([eigen_inverse, matmul(eigen_inverse, vert_deriv)]))
    leave_adjoint = wide(jnp.stack([inverse_t, -matmul(deriv_t, inverse_t)]))
    leave_forward = wide(-jnp.stack([eigen_vectors, matmul(vert_deriv, eigen_vectors)]))
    slope = wide(vert_deriv)

    a_one = into_levels(cotangent, eigen_vectors, (1,), count_x)
    a_two = into_levels(
        cotangent,
        enter_adjoint,
        (0, 2),
        count_x,
        a_one,
        enter_forward,
        leave_adjoint,
        leave_forward,
        slope,
        profile,
    )
    low, high, first, final = edges_of(velocity, a_one)
    sides = (shifted(final, "gx", 1), shifted(first, "gx", -1))
    lanes = -(-velocity.shape[1] // 128) * 128
    edges = [
        jnp.pad(edge, ((0, 0), (0, 0), (0, lanes - edge.shape[2])))
        for edge in (shifted(high, "gy", 1), shifted(low, "gy", -1))
    ]
    a_one = swap_x(a_one)
    a_sloped = x_forward(me, a_one, table_plain, *sides, *edges)
    a_two = swap_x(*gate([a_two], [a_one]))
    common = (velocity, sides, edges, coefficient, profile, slope)
    section, laplace, f_one = make_section(
        *common, enter_forward, count_x, (1,), (), (a_sloped[0],)
    )
    section, laplace, f_two = make_section(
        *common, enter_forward, count_x, (0, 2), (section, laplace), ()
    )
    a_sloped = swap_y(a_sloped, ())
    a_plain = x_forward(me, a_two, table_joint, f_two)
    f_one = swap_x(*gate([f_one], [a_plain[0], *a_sloped]))
    a_plain = swap_y(a_plain, a_sloped)
    f_sloped = x_forward(me, f_one, table_plain, *a_sloped)
    f_two = swap_x(*gate([f_two], [f_one]))
    f_sloped = swap_y(f_sloped, a_plain)
    f_plain = x_forward(me, f_two, table_joint, *a_plain)

    def solve(plain, sloped, follow):
        full = (full_x, full_y)
        return y_solve(plain, sloped, rates, me, y_forward, y_inverse, full, follow)

    a_flat, a_bent = solve(a_plain, a_sloped, f_plain[0])
    f_plain = swap_y(f_plain, f_sloped)
    a_flat = swap_y(a_flat, f_plain)
    f_flat, f_bent = solve(f_plain, f_sloped, a_bent[0])
    f_flat = swap_y(f_flat, a_flat, early=False)
    a_two = x_inverse(me, a_flat, back_joint, count_x, f_flat[0])
    a_bent = swap_y(a_bent, f_flat, (a_two,), False)
    a_two = swap_x(a_two)
    f_two = x_inverse(me, f_flat, back_joint, count_x, a_bent[0])
    adjoint = from_levels(a_two, leave_adjoint, cotangent, (0, 2), False)
    f_bent = swap_y(f_bent, a_bent, (adjoint,), False)
    f_two = swap_x(*gate([f_two], [a_two]))
    a_one = x_inverse(me, a_bent, back_plain, count_x, f_bent[0], 10)
    (a_one,) = gate([a_one], [f_two])
    f_one = x_inverse(me, f_bent, back_plain, count_x, a_one)
    a_one = swap_x(a_one)
    f_one = swap_x(*gate([f_one], [a_one]))

    adjoint_velocity, gradient = gradient_of(
        a_one, leave_adjoint, cotangent, adjoint, laplace, profile, f_bent[1]
    )
    new_velocity = from_levels(f_two, leave_forward, section, (0, 2), True, a_one)
    new_velocity = from_levels(f_one, leave_forward, new_velocity, (1,), True)
    return (new_velocity, adjoint_velocity, gradient)


def solution(mesh):
    in_specs = (
        P(None, "gx", None, "gy"),
        P(None, "gx", None, "gy"),
        P("gx", None, "gy"),
        P(),
        P(),
        P(),
        P(),
        P(),
    )
    out_specs = (P(None, "gx", None, "gy"), P(None, "gx", None, "gy"), P("gx", None, "gy"))
    return jax.shard_map(body, mesh=mesh, in_specs=in_specs, out_specs=out_specs, check_vma=False)
```

```python
import functools
import math

import jax
import jax.numpy as jnp
import numpy as np
from jax import lax
from jax.experimental import pallas as pl
from jax.experimental.pallas import tpu as pltpu
from jax.sharding import PartitionSpec as P

step_weight = 0.3 * 8.0 / 15.0
precise = lax.Precision.HIGHEST
half = jnp.bfloat16
vmem_bytes = 60 * 1024 * 1024


def line_transform(count):
    modes = count // 2
    points = np.arange(count)
    angle = (np.arange(modes)[:, None] * points[None, :] % count) * (2.0 * np.pi / count)
    real = np.cos(angle)
    imag = -np.sin(angle)
    imag[0] = np.where(points % 2 == 0, 1.0, -1.0)
    scale = np.full((modes, 1), 2.0 / count)
    scale[0] = 1.0 / count
    wave = (np.arange(modes) * (2.0 * np.pi / count))[:, None]
    forward = np.stack([real, imag])
    forward_slope = np.stack([-wave * imag, wave * real])
    inverse = np.stack([scale * real, scale * imag])
    inverse_slope = np.stack([scale * wave * imag, -scale * wave * real])
    return forward, forward_slope, inverse, inverse_slope


def grouped(table, groups):
    parts, modes, points = table.shape
    split = table.reshape(parts, groups, modes // groups, points)
    return np.swapaxes(split, 0, 1).reshape(groups, parts * modes // groups, points)


def halves(table):
    table = table.astype(np.float32)
    high = table.astype(half)
    low = (table - high.astype(np.float32)).astype(half)
    return np.stack([high, low])


def split(values):
    high = values.astype(half)
    low = (values - high.astype(jnp.float32)).astype(half)
    return high, low


def product(left, right):
    def dot(a, b):
        return jnp.dot(a, b, preferred_element_type=jnp.float32)

    return dot(left[0], right[0]) + (dot(left[0], right[1]) + dot(left[1], right[0]))


def parameters(flops, read, written, weight=100):
    return dict(
        compiler_params=pltpu.CompilerParams(vmem_limit_bytes=vmem_bytes),
        cost_estimate=pl.CostEstimate(
            flops=weight * flops, bytes_accessed=4 * weight * (read + written), transcendentals=0
        ),
    )


def block_x(part_x):
    return 16 if part_x % 16 == 0 else 8


def wide(matrix):
    high = lax.reduce_precision(matrix, exponent_bits=8, mantissa_bits=7)
    low = (matrix - high).astype(half)
    high = high.astype(half)
    return jnp.concatenate([high, high, low], axis=-1)


def narrow_product(matrix, field):
    high, low = split(field)
    return jnp.dot(
        matrix, jnp.concatenate([high, low, high], axis=0), preferred_element_type=jnp.float32
    )


anywhere = pl.BlockSpec(memory_space=pl.ANY)
scalars = pl.BlockSpec(memory_space=pltpu.SMEM)


def into_kernel(plain, field_ref, matrix_ref, *refs):
    out_ref, rows_ref = refs[-2:]
    sublanes, levels, part_y = field_ref.shape[1:]
    if plain:
        matrix = -matrix_ref[...]
        high = matrix.astype(half).astype(jnp.float32)
        matrix = jnp.concatenate([high, high, matrix - high], axis=0).T.astype(half)
    else:
        matrix = matrix_ref[0]
    for pair in range(0, sublanes, 2):
        fields = jnp.concatenate([field_ref[0, pair], field_ref[0, pair + 1]], axis=1)
        turned = narrow_product(matrix, fields)
        for x in (pair, pair + 1):
            rows_ref[pl.ds(x, levels, stride=sublanes), :] = turned[
                :, (x - pair) * part_y : (x - pair + 1) * part_y
            ]
    out_ref[...] = rows_ref[...].reshape(out_ref.shape)


def into_levels(fields, matrices, components, groups, *follow):
    _, part_x, levels, part_y = fields.shape
    sublanes = block_x(part_x)
    count = len(components)
    plain = matrices.ndim == 2
    per = levels // groups
    first, step = components[0], (components[1] - components[0] if count > 1 else 1)
    size = count * part_x * levels * part_y
    return pl.pallas_call(
        functools.partial(into_kernel, plain),
        grid=(count, part_x // sublanes),
        in_specs=[
            pl.BlockSpec(
                (1, sublanes, levels, part_y), lambda f, i: (first + f * step, i, 0, 0)
            ),
            pl.BlockSpec((levels, levels), lambda f, i: (0, 0))
            if plain
            else pl.BlockSpec((1, levels, 3 * levels), lambda f, i: (f, 0, 0)),
        ]
        + [anywhere] * len(follow),
        out_specs=pl.BlockSpec((groups, 1, per, sublanes, part_y), lambda f, i: (0, f, 0, i, 0)),
        out_shape=jax.ShapeDtypeStruct((groups, count, per, part_x, part_y), jnp.float32),
        scratch_shapes=[pltpu.VMEM((levels * sublanes, part_y), jnp.float32)],
        name="into_levels",
        **parameters(6 * size * levels, size, size),
    )(fields, matrices, *follow)


def edges_kernel(field_ref, _, low_ref, high_ref, first_ref, last_ref):
    sublanes, levels, part_y = field_ref.shape[1:]
    step = pl.program_id(0)
    lane = lax.broadcasted_iota(jnp.int32, (levels, low_ref.shape[2]), 1)
    for c in range(3):
        low = low_ref[c]
        high = high_ref[c]
        for x in range(sublanes):
            here = lane == step * sublanes + x
            low = jnp.where(here, field_ref[c, x, :, 0:1], low)
            high = jnp.where(here, field_ref[c, x, :, part_y - 1 : part_y], high)
        low_ref[c] = low
        high_ref[c] = high

    @pl.when(step == 0)
    def _():
        first_ref[...] = field_ref[:, 0:1]

    @pl.when(step == pl.num_programs(0) - 1)
    def _():
        last_ref[...] = field_ref[:, sublanes - 1 :]


def edges_of(field, follow):
    _, part_x, levels, part_y = field.shape
    sublanes = block_x(part_x)
    size = part_x * levels * part_y
    shapes = [(3, levels, part_x)] * 2 + [(3, 1, levels, part_y)] * 2
    return pl.pallas_call(
        edges_kernel,
        grid=(part_x // sublanes,),
        in_specs=[
            pl.BlockSpec((3, sublanes, levels, part_y), lambda i: (0, i, 0, 0)),
            anywhere,
        ],
        out_specs=[pl.BlockSpec(shapes[0], lambda i: (0, 0, 0))] * 2
        + [pl.BlockSpec(shapes[2], lambda i: (0, 0, 0, 0))] * 2,
        out_shape=[jax.ShapeDtypeStruct(shape, jnp.float32) for shape in shapes],
        name="edges_of",
        **parameters(0, 3 * size, 0),
    )(field, follow)


def section_kernel(*refs):
    field_ref, own_ref, before_ref, after_ref, west_ref, east_ref, south_ref, north_ref = refs[:8]
    coefficient_ref, profile_ref, deriv_ref, matrix_ref = refs[8:12]
    section_ref, laplace_ref, out_ref, rows_ref = refs[-4:]
    sublanes, levels, part_y = field_ref.shape[1:]
    edges = south_ref.shape[2]
    step = pl.program_id(1)
    last = pl.num_programs(1) - 1
    lane = lax.broadcasted_iota(jnp.int32, (levels, part_y), 1)
    profile = step_weight * profile_ref[...]
    for pair in range(0, sublanes, 2):
        own = jnp.concatenate([own_ref[0, pair], own_ref[0, pair + 1]], axis=1)
        slopes = narrow_product(deriv_ref[...], own)
        sections = []
        for x in (pair, pair + 1):
            place = step * sublanes + x
            field = own_ref[0, x]
            if x == 0:
                west = jnp.where(step == 0, west_ref[0, 0], before_ref[0, 0])
            else:
                west = own_ref[0, x - 1]
            if x == sublanes - 1:
                east = jnp.where(step == last, east_ref[0, 0], after_ref[0, 0])
            else:
                east = own_ref[0, x + 1]
            low = pltpu.roll(south_ref[0], lax.rem(edges - place, edges), 1)[:, :part_y]
            high = pltpu.roll(north_ref[0], lax.rem(edges + part_y - 1 - place, edges), 1)
            south = jnp.where(lane == 0, low, pltpu.roll(field, 1, 1))
            north = jnp.where(
                lane == part_y - 1, high[:, :part_y], pltpu.roll(field, part_y - 1, 1)
            )
            laplace = east + west + north + south - 4.0 * field
            slope_z = slopes[:, (x - pair) * part_y : (x - pair + 1) * part_y]
            advect = (0.5 * field_ref[0, x]) * (east - west)
            advect = advect + (0.5 * field_ref[1, x]) * (north - south)
            advect = advect + field_ref[2, x] * slope_z
            viscosity = profile * coefficient_ref[x]
            section = field + (viscosity * laplace - step_weight * advect)
            laplace_ref[0, x] = laplace
            section_ref[0, x] = section
            sections.append(section)
        turned = narrow_product(matrix_ref[0], jnp.concatenate(sections, axis=1))
        for x in (pair, pair + 1):
            rows_ref[pl.ds(x, levels, stride=sublanes), :] = turned[
                :, (x - pair) * part_y : (x - pair + 1) * part_y
            ]
    out_ref[...] = rows_ref[...].reshape(out_ref.shape)


def make_section(
    field, sides, edges, coefficient, profile, deriv, matrices, groups, components, done, follow
):
    _, part_x, levels, part_y = field.shape
    sublanes = block_x(part_x)
    per = levels // groups
    count = len(components)
    first, step = components[0], (components[1] - components[0] if count > 1 else 1)
    size = count * part_x * levels * part_y
    whole = pl.BlockSpec((3, sublanes, levels, part_y), lambda f, i: (0, i, 0, 0))
    own = pl.BlockSpec((1, sublanes, levels, part_y), lambda f, i: (first + f * step, i, 0, 0))
    plane = (1, 1, levels, part_y)
    fixed = pl.BlockSpec(plane, lambda f, i: (first + f * step, 0, 0, 0))
    edge = pl.BlockSpec((1, *edges[0].shape[1:]), lambda f, i: (first + f * step, 0, 0))
    full = jax.ShapeDtypeStruct(field.shape, jnp.float32)
    return pl.pallas_call(
        section_kernel,
        grid=(count, part_x // sublanes),
        in_specs=[
            whole,
            own,
            pl.BlockSpec(
                plane, lambda f, i: (first + f * step, jnp.maximum(i * sublanes - 1, 0), 0, 0)
            ),
            pl.BlockSpec(
                plane,
                lambda f, i: (
                    first + f * step,
                    jnp.minimum((i + 1) * sublanes, part_x - 1),
                    0,
                    0,
                ),
            ),
            fixed,
            fixed,
            edge,
            edge,
            pl.BlockSpec((sublanes, levels, part_y), lambda f, i: (i, 0, 0)),
            pl.BlockSpec((levels, part_y), lambda f, i: (0, 0)),
            pl.BlockSpec((levels, 3 * levels), lambda f, i: (0, 0)),
            pl.BlockSpec((1, levels, 3 * levels), lambda f, i: (f, 0, 0)),
        ]
        + [anywhere] * (len(done) + len(follow)),
        out_specs=[
            own,
            own,
            pl.BlockSpec((groups, 1, per, sublanes, part_y), lambda f, i: (0, f, 0, i, 0)),
        ],
        out_shape=[
            full,
            full,
            jax.ShapeDtypeStruct((groups, count, per, part_x, part_y), jnp.float32),
        ],
        input_output_aliases={12 + i: i for i in range(len(done))},
        scratch_shapes=[pltpu.VMEM((levels * sublanes, part_y), jnp.float32)],
        name="make_section",
        **parameters(12 * size * levels, 6 * size, 3 * size),
    )(
        field,
        field,
        field,
        field,
        *sides,
        *edges,
        coefficient,
        profile,
        deriv,
        matrices,
        *done,
        *follow,
    )


def x_kernel(me_ref, rows_ref, table_ref, *refs):
    targets = table_ref.shape[1]
    out_refs = refs[-targets:]
    groups, count, block, part_x, part_y = rows_ref.shape
    columns = []
    for m in range(block):
        lines = [rows_ref[:, f, m].reshape(groups * part_x, part_y) for f in range(count)]
        columns.append(jnp.concatenate(lines, axis=0))
    data = split(jnp.concatenate(columns, axis=1))
    order = [lax.rem(me_ref[0] + s, targets) for s in range(targets)]
    spectrum = product(
        [jnp.concatenate([table_ref[h, o] for o in order], axis=0) for h in range(2)], data
    )
    lines = table_ref.shape[2]
    for s, out_ref in enumerate(out_refs):
        for m in range(block):
            out_ref[m] = spectrum[
                s * lines : (s + 1) * lines, m * part_y : (m + 1) * part_y
            ]


def block_of(levels):
    return 2 if levels % 2 == 0 else 1


def x_forward(me, rows, table, *follow):
    groups, count, levels, part_x, part_y = rows.shape
    targets, lines, depth = table.shape[1:]
    block = block_of(levels)
    size = groups * count * levels * part_x * part_y
    return pl.pallas_call(
        x_kernel,
        grid=(levels // block,),
        in_specs=[
            scalars,
            pl.BlockSpec((groups, count, block, part_x, part_y), lambda i: (0, 0, i, 0, 0)),
            pl.BlockSpec(table.shape, lambda i: (0, 0, 0, 0)),
        ]
        + [anywhere] * len(follow),
        out_specs=[pl.BlockSpec((block, lines, part_y), lambda i: (i, 0, 0))] * targets,
        out_shape=[jax.ShapeDtypeStruct((levels, lines, part_y), jnp.float32)] * targets,
        name="x_forward",
        **parameters(6 * size * targets * lines, size + table.size // 2, size // count),
    )(me, rows, table, *follow)


def solve_kernel(sources, full, group_ref, rates_ref, _, *refs):
    full_x, full_y = full
    in_refs = refs[: 2 * sources]
    forward_ref, inverse_ref = refs[2 * sources : 2 * sources + 2]
    out_refs = refs[2 * sources + 2 :]
    block, lines, part_y = in_refs[0].shape
    me = group_ref[0]
    data = split(
        jnp.concatenate([ref[...].reshape(block * lines, part_y) for ref in in_refs], axis=1)
    )
    origins = [lax.rem(me + sources - s, sources) for s in range(sources)]
    diverg = product(
        data,
        [
            jnp.concatenate([forward_ref[h, p, o] for p in range(2) for o in origins], axis=0)
            for h in range(2)
        ],
    )
    shape = (lines, full_y)
    pairs = lines // 2
    mode_x = me * pairs + lax.broadcasted_iota(jnp.int32, shape, 0) % pairs
    mode_y = lax.broadcasted_iota(jnp.int32, shape, 1) % (full_y // 2)
    wave_x = mode_x.astype(jnp.float32) * (2.0 * math.pi / full_x)
    wave_y = mode_y.astype(jnp.float32) * (2.0 * math.pi / full_y)
    squares = wave_x * wave_x + wave_y * wave_y
    solved = []
    for m in range(block):
        rate = rates_ref[pl.program_id(0) * block + m]
        solved.append(-diverg[m * lines : (m + 1) * lines] / (rate + squares))
    solved = split(jnp.concatenate(solved, axis=0))
    for s, out_ref in enumerate(out_refs):
        place = (s // sources, lax.rem(me + s, sources))
        result = product(solved, (inverse_ref[(0, *place)], inverse_ref[(1, *place)]))
        out_ref[...] = result.reshape(block, lines, part_y)


def y_solve(plain, sloped, rates, group, forward, inverse, full, follow):
    levels, lines, part_y = plain[0].shape
    sources = len(plain)
    block = block_of(levels)
    size = levels * lines * part_y * sources
    targets = 2 * sources
    spec = pl.BlockSpec((block, lines, part_y), lambda i: (i, 0, 0))
    fixed = pl.BlockSpec(forward.shape, lambda i: (0, 0, 0, 0, 0))
    outs = pl.pallas_call(
        functools.partial(solve_kernel, sources, full),
        grid=(levels // block,),
        in_specs=[scalars, scalars, anywhere]
        + [spec] * (2 * sources)
        + [fixed, pl.BlockSpec(inverse.shape, lambda i: (0, 0, 0, 0, 0))],
        out_specs=[spec] * targets,
        out_shape=[jax.ShapeDtypeStruct((levels, lines, part_y), jnp.float32)] * targets,
        name="y_solve",
        **parameters(
            24 * size * full[1], 2 * size + forward.size // 2 + inverse.size // 2, 2 * size
        ),
    )(group, rates, follow, *plain, *sloped, forward, inverse)
    return outs[:sources], outs[sources:]


def x_inverse_kernel(sources, me_ref, _, *refs):
    in_refs = refs[:sources]
    table_ref, out_ref, high_ref, low_ref, rows_ref = refs[sources:]
    _, _, part_x, levels, part_y = out_ref.shape

    @pl.when((pl.program_id(0) == 0) & (pl.program_id(1) == 0))
    def _():
        for m in range(levels):
            high, low = split(jnp.concatenate([ref[m] for ref in in_refs], axis=0))
            high_ref[:, m * part_y : (m + 1) * part_y] = high
            low_ref[:, m * part_y : (m + 1) * part_y] = low

    origins = [lax.rem(me_ref[0] + sources - s, sources) for s in range(sources)]
    table = [
        jnp.concatenate([table_ref[h, 0, o] for o in origins], axis=1) for h in range(2)
    ]
    lines = table[0].shape[0]
    block = block_of(levels)
    for start in range(0, levels, block):
        cut = slice(start * part_y, (start + block) * part_y)
        result = product(table, (high_ref[:, cut], low_ref[:, cut]))
        for m in range(block):
            rows_ref[pl.ds(start + m, lines, stride=levels), :] = result[
                :, m * part_y : (m + 1) * part_y
            ]
    out_ref[...] = rows_ref[...].reshape(out_ref.shape)


def x_inverse(me, pieces, table, groups, follow, weight=100):
    sources = len(pieces)
    levels, lines, part_y = pieces[0].shape
    count, full_x = table.shape[1], table.shape[3]
    part_x = full_x // groups
    steps = 1
    rows = full_x // steps
    size = levels * full_x * part_y
    return pl.pallas_call(
        functools.partial(x_inverse_kernel, sources),
        grid=(count, steps),
        in_specs=[scalars, anywhere]
        + [pl.BlockSpec((levels, lines, part_y), lambda f, i: (0, 0, 0))] * sources
        + [pl.BlockSpec((2, 1, sources, rows, lines), lambda f, i: (0, f, 0, i, 0))],
        out_specs=pl.BlockSpec(
            (groups // steps, 1, part_x, levels, part_y), lambda f, i: (i, f, 0, 0, 0)
        ),
        out_shape=jax.ShapeDtypeStruct((groups, count, part_x, levels, part_y), jnp.float32),
        scratch_shapes=[pltpu.VMEM((full_x, levels * part_y), half)] * 2
        + [pltpu.VMEM((rows * levels, part_y), jnp.float32)],
        name="x_inverse",
        **parameters(
            6 * size * full_x * count, size + table.size // 2, size * count, weight
        ),
    )(me, follow, *pieces, table)


def column(rows_ref, component, x):
    groups = rows_ref.shape[0]
    return jnp.concatenate([rows_ref[g, component, x] for g in range(groups)], axis=0)


def from_kernel(rows_ref, matrix_ref, base_ref, *refs):
    out_ref = refs[-1]
    part_y = base_ref.shape[3]
    for pair in range(0, base_ref.shape[1], 2):
        fields = [column(rows_ref, 0, x) for x in (pair, pair + 1)]
        turned = narrow_product(matrix_ref[0], jnp.concatenate(fields, axis=1))
        out_ref[0, pair] = base_ref[0, pair] + turned[:, :part_y]
        out_ref[0, pair + 1] = base_ref[0, pair + 1] + turned[:, part_y:]


def from_levels(rows, matrices, base, components, in_place, *follow):
    groups, count, part_x, per, part_y = rows.shape
    levels = groups * per
    sublanes = block_x(part_x)
    first, step = components[0], (components[1] - components[0] if count > 1 else 1)
    size = count * part_x * levels * part_y
    spec = pl.BlockSpec((1, sublanes, levels, part_y), lambda f, i: (first + f * step, i, 0, 0))
    return pl.pallas_call(
        from_kernel,
        grid=(count, part_x // sublanes),
        in_specs=[
            pl.BlockSpec((groups, 1, sublanes, per, part_y), lambda f, i: (0, f, i, 0, 0)),
            pl.BlockSpec((1, levels, 3 * levels), lambda f, i: (f, 0, 0)),
            spec,
        ]
        + [anywhere] * len(follow),
        out_specs=spec,
        out_shape=jax.ShapeDtypeStruct(base.shape, jnp.float32),
        input_output_aliases={2: 0} if in_place else {},
        name="from_levels",
        **parameters(6 * size * levels, 2 * size, size),
    )(rows, matrices, base, *follow)


def gradient_kernel(
    rows_ref, matrix_ref, base_ref, done_ref, laplace_ref, profile_ref, _, out_ref, gradient_ref
):
    profile = step_weight * profile_ref[...]
    part_y = base_ref.shape[3]
    for pair in range(0, base_ref.shape[1], 2):
        fields = [column(rows_ref, 0, x) for x in (pair, pair + 1)]
        turned = narrow_product(matrix_ref[0], jnp.concatenate(fields, axis=1))
        for x in (pair, pair + 1):
            value = base_ref[0, x] + turned[:, (x - pair) * part_y : (x - pair + 1) * part_y]
            first, last = done_ref[0, x], done_ref[2, x]
            out_ref[0, x], out_ref[1, x], out_ref[2, x] = first, value, last
            total = first * laplace_ref[0, x] + value * laplace_ref[1, x]
            gradient_ref[x] = profile * (total + last * laplace_ref[2, x])


def gradient_of(rows, matrix, base, done, laplace, profile, follow):
    groups, _, part_x, per, part_y = rows.shape
    levels = groups * per
    sublanes = block_x(part_x)
    size = part_x * levels * part_y

    whole = pl.BlockSpec((3, sublanes, levels, part_y), lambda i: (0, i, 0, 0))
    return pl.pallas_call(
        gradient_kernel,
        grid=(part_x // sublanes,),
        in_specs=[
            pl.BlockSpec((groups, 1, sublanes, per, part_y), lambda i: (0, 0, i, 0, 0)),
            pl.BlockSpec((1, levels, 3 * levels), lambda i: (0, 0, 0)),
            pl.BlockSpec((1, sublanes, levels, part_y), lambda i: (1, i, 0, 0)),
            whole,
            whole,
            pl.BlockSpec((levels, part_y), lambda i: (0, 0)),
            anywhere,
        ],
        out_specs=[whole, pl.BlockSpec((sublanes, levels, part_y), lambda i: (i, 0, 0))],
        out_shape=[
            jax.ShapeDtypeStruct(base.shape, jnp.float32),
            jax.ShapeDtypeStruct(base.shape[1:], jnp.float32),
        ],
        input_output_aliases={3: 0},
        name="gradient_of",
        **parameters(6 * size * levels, 7 * size, 2 * size),
    )(rows, matrix, base, done, laplace, profile, follow)


def shifted(cells, axis, shift):
    count = lax.axis_size(axis)
    return lax.ppermute(cells, axis, [(i, (i + shift) % count) for i in range(count)])


def swap_x(rows):
    return lax.all_to_all(rows, "gx", split_axis=0, concat_axis=0, tiled=True)


def gate_kernel(*refs):
    del refs


def gate(pieces, before, weight=0):
    count = len(pieces)
    return pl.pallas_call(
        gate_kernel,
        in_specs=[anywhere] * (count + len(before)),
        out_specs=[anywhere] * count,
        out_shape=[jax.ShapeDtypeStruct(p.shape, p.dtype) for p in pieces],
        input_output_aliases={i: i for i in range(count)},
        cost_estimate=pl.CostEstimate(
            flops=0, bytes_accessed=weight * pieces[0].size, transcendentals=0
        ),
        name="gate",
    )(*pieces, *before)


def swap_y(pieces, last, before=(), early=True):
    own, *sent = pieces
    if last:
        cut = 1 if early else len(sent)
        sent = [
            *gate(sent[:cut], [*last[1 : 1 + cut], *before]),
            *(gate(sent[cut:], last[1 + cut :]) if early else ()),
        ]
    return [own] + [shifted(piece, "gy", s) for s, piece in enumerate(sent, 1)]


def matmul(a, b):
    return jnp.dot(a, b, precision=precise)


def body(
    velocity,
    cotangent,
    coefficient,
    level_profile,
    vert_deriv,
    eigen_vectors,
    eigen_inverse,
    eigen_rates,
):
    count_x = lax.axis_size("gx")
    count_y = lax.axis_size("gy")
    full_x = count_x * velocity.shape[1]
    full_y = count_y * velocity.shape[3]
    per = velocity.shape[2] // count_x
    me = lax.axis_index("gy").astype(jnp.int32).reshape(1)
    rates = lax.dynamic_slice_in_dim(eigen_rates, lax.axis_index("gx") * per, per)

    forward, forward_slope, inverse, inverse_slope = line_transform(full_x)
    plain_x = grouped(forward, count_y)
    joint_x = np.concatenate([grouped(forward_slope, count_y), plain_x], axis=2)
    table_plain, table_joint = halves(plain_x), halves(joint_x)

    def columns(*tables):
        turned = [np.swapaxes(grouped(table, count_y), 1, 2) for table in tables]
        return halves(np.stack(turned))

    back_plain, back_joint = columns(inverse), columns(inverse_slope, inverse)

    forward, forward_slope, inverse, inverse_slope = line_transform(full_y)

    def points(table):
        return table.reshape(full_y, count_y, full_y // count_y).transpose(1, 2, 0)

    y_forward = halves(np.stack([points(forward), points(forward_slope)]))
    y_inverse = halves(
        np.stack([np.swapaxes(points(table), 1, 2) for table in (inverse, inverse_slope)])
    )

    vectors_t = eigen_vectors.T
    inverse_t = eigen_inverse.T
    deriv_t = vert_deriv.T
    profile = jnp.broadcast_to(level_profile[:, None], velocity.shape[2:])
    enter_adjoint = wide(jnp.stack([-vectors_t, matmul(vectors_t, deriv_t)]))
    enter_forward = wide(jnp.stack([eigen_inverse, matmul(eigen_inverse, vert_deriv)]))
    leave_adjoint = wide(jnp.stack([inverse_t, -matmul(deriv_t, inverse_t)]))
    leave_forward = wide(-jnp.stack([eigen_vectors, matmul(vert_deriv, eigen_vectors)]))
    slope = wide(vert_deriv)

    a_one = into_levels(cotangent, eigen_vectors, (1,), count_x)
    a_two = into_levels(
        cotangent,
        enter_adjoint,
        (0, 2),
        count_x,
        a_one,
        enter_forward,
        leave_adjoint,
        leave_forward,
        slope,
        profile,
    )
    low, high, first, final = edges_of(velocity, a_one)
    sides = (shifted(final, "gx", 1), shifted(first, "gx", -1))
    lanes = -(-velocity.shape[1] // 128) * 128
    edges = [
        jnp.pad(edge, ((0, 0), (0, 0), (0, lanes - edge.shape[2])))
        for edge in (shifted(high, "gy", 1), shifted(low, "gy", -1))
    ]
    a_one = swap_x(a_one)
    a_sloped = x_forward(me, a_one, table_plain, *sides, *edges)
    a_two = swap_x(*gate([a_two], [a_one]))
    common = (velocity, sides, edges, coefficient, profile, slope)
    section, laplace, f_one = make_section(
        *common, enter_forward, count_x, (1,), (), (a_sloped[0],)
    )
    section, laplace, f_two = make_section(
        *common, enter_forward, count_x, (0, 2), (section, laplace), ()
    )
    a_sloped = swap_y(a_sloped, ())
    a_plain = x_forward(me, a_two, table_joint, f_two)
    f_one = swap_x(*gate([f_one], [a_plain[0], *a_sloped]))
    a_plain = swap_y(a_plain, a_sloped)
    f_sloped = x_forward(me, f_one, table_plain, *a_sloped)
    f_two = swap_x(*gate([f_two], [f_one]))
    f_sloped = swap_y(f_sloped, a_plain)
    f_plain = x_forward(me, f_two, table_joint, *a_plain)

    def solve(plain, sloped, follow):
        full = (full_x, full_y)
        return y_solve(plain, sloped, rates, me, y_forward, y_inverse, full, follow)

    a_flat, a_bent = solve(a_plain, a_sloped, f_plain[0])
    f_plain = swap_y(f_plain, f_sloped)
    a_flat = swap_y(a_flat, f_plain)
    f_flat, f_bent = solve(f_plain, f_sloped, a_bent[0])
    f_flat = swap_y(f_flat, a_flat, early=False)
    a_two = x_inverse(me, a_flat, back_joint, count_x, f_flat[0])
    a_bent = swap_y(a_bent, f_flat, (a_two,), False)
    a_two = swap_x(a_two)
    f_two = x_inverse(me, f_flat, back_joint, count_x, a_bent[0])
    adjoint = from_levels(a_two, leave_adjoint, cotangent, (0, 2), False)
    f_bent = swap_y(f_bent, a_bent, (adjoint,), False)
    f_two = swap_x(*gate([f_two], [a_two]))
    a_one = x_inverse(me, a_bent, back_plain, count_x, f_bent[0], 10)
    (a_one,) = gate([a_one], [f_two])
    f_one = x_inverse(me, f_bent, back_plain, count_x, a_one)
    a_one = swap_x(a_one)
    f_one = swap_x(*gate([f_one], [a_one]))

    adjoint_velocity, gradient = gradient_of(
        a_one, leave_adjoint, cotangent, adjoint, laplace, profile, f_bent[1]
    )
    new_velocity = from_levels(f_two, leave_forward, section, (0, 2), True, a_one)
    new_velocity = from_levels(f_one, leave_forward, new_velocity, (1,), True)
    return (new_velocity, adjoint_velocity, gradient)


def solution(mesh):
    in_specs = (
        P(None, "gx", None, "gy"),
        P(None, "gx", None, "gy"),
        P("gx", None, "gy"),
        P(),
        P(),
        P(),
        P(),
        P(),
    )
    out_specs = (P(None, "gx", None, "gy"), P(None, "gx", None, "gy"), P("gx", None, "gy"))
    return jax.shard_map(body, mesh=mesh, in_specs=in_specs, out_specs=out_specs, check_vma=False)
```
